128 devices in a mesh: cp: 32 (over z, x, core), hd: 4 (over y).
Axes of the slice: x: 4, y: 4, z: 4, core: 2. Of those that a mesh axis runs over, the one named last changes fastest.
Arguments:
- queries: bfloat16 [8192, 8192], P(('cp', 'hd')), may hold values from -3 to 3
- keys: bfloat16 [8192, 1024], P(('cp', 'hd')), may hold values from -3 to 3
- values: bfloat16 [8192, 1024], P(('cp', 'hd')), may hold values from -4 to 4
- fwd_out: bfloat16 [8192, 8192], P(('cp', 'hd')), may hold values from -4 to 4
- out_grad: bfloat16 [8192, 8192], P(('cp', 'hd')), may hold values from -4 to 4
- log_norm: float32 [8192, 64], P('cp', 'hd'), may hold values from 4 to 7
- doc_bounds: int32 [12], replicated, may hold values from 0 to 8192, as said below
- span_plan: int32 [32, 2], replicated, may hold values from 0 to 63, as said below
- read_lists: int32 [32, 2, 16], P('cp'), may hold values from -1 to 63, as said below
Outputs:
- grad_queries: bfloat16 [8192, 8192], P(('cp', 'hd'))
- grad_keys: bfloat16 [8192, 1024], P(('cp', 'hd'))
- grad_values: bfloat16 [8192, 1024], P(('cp', 'hd'))
The draws below stay inside these ranges and needn't reach their ends.
Inputs may be any that keep to these rules, and one draw needn't show every extreme that they name: `doc_bounds`: rises from 0 to 8192; the first document has 127 tokens, the second exactly 1794, every later one 512 to 1794. `span_plan`: every span stands in exactly one slot. `read_lists`: for the span c in slot j of rank r: the spans from the one holding the start of the document of c's first token up to c, ascending, then -1 in the remaining entries; the number of spans is at most 16, and exactly 16 for span 16 - 1.
All inputs are finite; a program needn't handle non-finite values.
Results may differ from the reference program's by a relative error of at most 0.0054.
Values may be sent and summed in bfloat16 or wider, within the bound.
No kernel may reach another device: no remote copies, remote signals or barrier semaphores. Data moves between devices by JAX's collectives and lax.ppermute only.
A program may use at most 128 MiB of HBM per device.

```python
import jax
import jax.numpy as jnp
from jax import lax

HEAD_DIM = 128
Q_HEADS = 64
KV_HEADS = 8
SPAN = 128
SPANS_DEV = 2
SPANS = 64
TOKENS = 8192
MAX_READ = 16
DOC_MOST = 1794
DOC_LEAST = 512
REST_DOCS = 9
DOCS = 11
N_CP = 32


def plan_tables(key):
    spare = TOKENS - (SPAN - 1) - DOC_MOST
    extra = spare - REST_DOCS * DOC_LEAST
    weights = jax.random.randint(key, (REST_DOCS,), 12, 20).astype(jnp.int32)
    lengths = DOC_LEAST + weights * extra // jnp.sum(weights)
    lengths = lengths.at[REST_DOCS - 1].add(spare - jnp.sum(lengths))
    leading = jnp.array([SPAN - 1, DOC_MOST], dtype=jnp.int32)
    all_lengths = jnp.concatenate([leading, lengths.astype(jnp.int32)])
    bounds = jnp.concatenate([jnp.zeros((1,), jnp.int32), jnp.cumsum(all_lengths).astype(jnp.int32)])
    firsts = jnp.arange(SPANS, dtype=jnp.int32) * SPAN
    doc_ids = jnp.sum((bounds[None, 1:] <= firsts[:, None]).astype(jnp.int32), axis=1)
    doc_range = jnp.arange(DOCS + 1, dtype=jnp.int32)
    starts = jnp.sum(jnp.where(doc_range[None, :] == doc_ids[:, None], bounds[None, :], 0), axis=1)
    begin_span = starts // SPAN
    read_counts = jnp.arange(SPANS, dtype=jnp.int32) - begin_span + 1
    read_steps = jnp.arange(MAX_READ, dtype=jnp.int32)
    read_table = jnp.where(read_steps[None, :] < read_counts[:, None], begin_span[:, None] + read_steps[None, :], -1).astype(jnp.int32)
    tie_breaks = jax.random.permutation(jax.random.fold_in(key, 7), SPANS).astype(jnp.int32)
    ordering = jnp.argsort(read_counts * SPANS + tie_breaks, stable=True).astype(jnp.int32)
    position = jnp.arange(SPANS, dtype=jnp.int32)
    rounds = position // N_CP
    within = position % N_CP
    owner = jnp.where(rounds % 2 == 0, within, N_CP - 1 - within)
    plan = jnp.zeros((N_CP, SPANS_DEV), jnp.int32).at[owner, rounds].set(ordering)
    return (bounds, plan, read_table[plan])


def draw_doc_bounds(key, part):
    return plan_tables(key)[0]


def draw_span_plan(key, part):
    return plan_tables(key)[1]


def draw_read_lists(key, part):
    return plan_tables(key)[2]


def steps_of(key, extent, shards, least, high):
    factor_of, own = 1.0, jax.random.fold_in(key, 6)
    for dim, parts in shards:
        draws = jnp.exp(jax.random.uniform(jax.random.fold_in(own, dim), (parts,), jnp.float32, least / len(shards), high / len(shards)))
        factor_of = factor_of * jnp.repeat(draws, extent[dim] // parts).reshape([-1 if axis == dim else 1 for axis in range(len(extent))])
    return factor_of


def noise(key, shape, deviation, reach, split=(), kind=jnp.bfloat16):
    values = jax.random.normal(key, shape, jnp.float32) * deviation
    if len(split) > 0:
        values = steps_of(key, shape, split, -0.22, 0.18) * values
    return jnp.clip(values, min=-reach, max=reach).astype(kind)


def setup_inputs(seed: int = 0) -> dict:
    key_of = jax.random.split(jax.random.key(seed), 10)
    return {
        "queries": noise(key_of[0], (TOKENS, Q_HEADS * HEAD_DIM), 1.0, 3.0, ((0, 128),)),
        "keys": noise(key_of[1], (TOKENS, KV_HEADS * HEAD_DIM), 1.0, 3.0, ((0, 128),)),
        "values": noise(key_of[2], (TOKENS, KV_HEADS * HEAD_DIM), 1.0, 4.0, ((0, 128),)),
        "fwd_out": noise(key_of[3], (TOKENS, Q_HEADS * HEAD_DIM), 1.0, 4.0, ((0, 128),)),
        "out_grad": noise(key_of[4], (TOKENS, Q_HEADS * HEAD_DIM), 1.0, 4.0, ((0, 128),)),
        "log_norm": jnp.clip(4.0 + 3.0 * jax.random.uniform(key_of[5], (TOKENS, Q_HEADS), jnp.float32) ** steps_of(key_of[5], (TOKENS, Q_HEADS), ((0, 32), (1, 4)), -0.2, 0.2), 4.0, 7.0),
        "doc_bounds": draw_doc_bounds(jax.random.fold_in(key_of[9], 71), 0),
        "span_plan": draw_span_plan(jax.random.fold_in(key_of[9], 71), 0),
        "read_lists": draw_read_lists(jax.random.fold_in(key_of[9], 71), 0),
    }


def doc_index(bounds, places):
    return jnp.sum((bounds[None, 1:] <= places[:, None]).astype(jnp.int32), axis=1)


def reference(queries, keys, values, fwd_out, out_grad, log_norm, doc_bounds, span_plan, read_lists):
    factor = HEAD_DIM ** -0.5
    repeat = Q_HEADS // KV_HEADS
    reads = read_lists.shape[2]
    plan_flat = span_plan.reshape(-1).astype(jnp.int32)
    read_table = read_lists.reshape(SPANS, reads).astype(jnp.int32)
    weighted = fwd_out.astype(jnp.float32) * out_grad.astype(jnp.float32)
    delta = jnp.sum(weighted.reshape(TOKENS, Q_HEADS, HEAD_DIM), axis=2)
    slot_of = jnp.zeros((SPANS,), jnp.int32).at[plan_flat].set(jnp.arange(SPANS, dtype=jnp.int32))
    query_blocks = queries.reshape(SPANS, SPAN, KV_HEADS, repeat, HEAD_DIM)
    grad_blocks = out_grad.reshape(SPANS, SPAN, KV_HEADS, repeat, HEAD_DIM)
    key_blocks = keys.reshape(SPANS, SPAN, KV_HEADS, HEAD_DIM)
    value_blocks = values.reshape(SPANS, SPAN, KV_HEADS, HEAD_DIM)
    lse_blocks = log_norm.reshape(SPANS, SPAN, KV_HEADS, repeat).transpose(0, 2, 3, 1)
    delta_blocks = delta.reshape(SPANS, SPAN, KV_HEADS, repeat).transpose(0, 2, 3, 1)
    offsets = jnp.arange(SPAN, dtype=jnp.int32)

    def per_slot(carry, slot_now):
        sums_k, sums_v = carry
        entries = read_table[slot_now]
        is_live = entries >= 0
        safe_span = jnp.where(is_live, entries, 0).astype(jnp.int32)
        key_slots = slot_of[safe_span]
        key_tiles = key_blocks[key_slots].reshape(reads * SPAN, KV_HEADS, HEAD_DIM).astype(jnp.float32)
        value_tiles = value_blocks[key_slots].reshape(reads * SPAN, KV_HEADS, HEAD_DIM).astype(jnp.float32)
        key_place = (safe_span[:, None] * SPAN + offsets[None, :]).reshape(-1)
        key_live = jnp.repeat(is_live, SPAN)
        query_place = plan_flat[slot_now] * SPAN + offsets
        query_doc = doc_index(doc_bounds, query_place)
        key_doc = doc_index(doc_bounds, key_place)
        query_tile = query_blocks[slot_now].astype(jnp.float32)
        grad_tile = grad_blocks[slot_now].astype(jnp.float32)
        scores = jnp.einsum("qgrd,kgd->grqk", query_tile, key_tiles) * factor
        allowed = (key_place[None, :] <= query_place[:, None]) & (key_doc[None, :] == query_doc[:, None]) & key_live[None, :]
        shifted = jnp.where(allowed, scores - lse_blocks[slot_now][..., None], 0.0)
        probs = jnp.where(allowed, jnp.exp(shifted), 0.0)
        dprob = jnp.einsum("qgrd,kgd->grqk", grad_tile, value_tiles)
        dscore = lax.optimization_barrier((probs * (dprob - delta_blocks[slot_now][..., None]) * factor).astype(jnp.bfloat16)).astype(jnp.float32)
        probs_low = lax.optimization_barrier(probs.astype(jnp.bfloat16)).astype(jnp.float32)
        part_v = jnp.einsum("grqk,qgrd->kgd", probs_low, grad_tile).reshape(reads, SPAN, KV_HEADS * HEAD_DIM)
        part_k = jnp.einsum("grqk,qgrd->kgd", dscore, query_tile).reshape(reads, SPAN, KV_HEADS * HEAD_DIM)
        part_q = jnp.einsum("grqk,kgd->qgrd", dscore, key_tiles).reshape(SPAN, Q_HEADS * HEAD_DIM)
        sums_k = sums_k.at[key_slots].add(part_k)
        sums_v = sums_v.at[key_slots].add(part_v)
        return (sums_k, sums_v), part_q

    empty = jnp.zeros((SPANS, SPAN, KV_HEADS * HEAD_DIM), jnp.float32)
    (sums_k, sums_v), grad_q = lax.scan(per_slot, (empty, empty), jnp.arange(SPANS, dtype=jnp.int32))
    grad_queries = grad_q.reshape(TOKENS, Q_HEADS * HEAD_DIM).astype(jnp.bfloat16)
    grad_keys = sums_k.reshape(TOKENS, KV_HEADS * HEAD_DIM).astype(jnp.bfloat16)
    grad_values = sums_v.reshape(TOKENS, KV_HEADS * HEAD_DIM).astype(jnp.bfloat16)
    return (grad_queries, grad_keys, grad_values)
```

```python
import jax
import jax.numpy as jnp
from jax import lax
from jax.experimental import pallas as pl
from jax.experimental.pallas import tpu as pltpu
from jax.sharding import Mesh, PartitionSpec as P

HEAD_DIM = 128
SPAN = 128
HALF = 64
SLAB = 2048
LANES = 512
PACKED = 528
ROWS = ("z", "x", "c", "y")
MIB = 1024 * 1024


def dot(a, b, ca, cb):
    return lax.dot_general(a, b, (((ca,), (cb,)), ((), ())), preferred_element_type=jnp.float32)


def pack_kv_kernel(keys_ref, values_ref, out_ref):
    for x in range(4):
        for y in range(4):
            cols = slice((2 * y + x // 2) * HEAD_DIM, (2 * y + x // 2 + 1) * HEAD_DIM)
            out_ref[x, 0, y] = keys_ref[:, cols]
            out_ref[x, 1, y] = values_ref[:, cols]


def pack_q_kernel(queries_ref, grad_ref, fwd_ref, out_ref):
    row = lax.broadcasted_iota(jnp.int32, (16, HEAD_DIM), 0)
    for x in range(4):
        delta = jnp.zeros((16, HALF), jnp.float32)
        for h in range(4):
            cols = slice((x * 4 + h) * HEAD_DIM, (x * 4 + h + 1) * HEAD_DIM)
            grad = grad_ref[:, cols]
            out_ref[x, 0, h * HALF : (h + 1) * HALF] = queries_ref[:, cols]
            out_ref[x, 0, 256 + h * HALF : 256 + (h + 1) * HALF] = grad
            product = grad.astype(jnp.float32) * fwd_ref[:, cols].astype(jnp.float32)
            high = product.astype(jnp.bfloat16)
            low = (product - high.astype(jnp.float32)).astype(jnp.bfloat16)
            pick = (row == h).astype(jnp.bfloat16)
            delta = delta + dot(pick, high, 1, 1) + dot(pick, low, 1, 1)
        high = delta.astype(jnp.bfloat16)
        low = (delta - high.astype(jnp.float32)).astype(jnp.bfloat16)
        out_ref[x, 0, 512:PACKED] = jnp.concatenate([high, low], axis=1)


def unpack_q_kernel(in_ref, out_ref):
    for x in range(4):
        for h in range(4):
            cols = slice((x * 4 + h) * HEAD_DIM, (x * 4 + h + 1) * HEAD_DIM)
            out_ref[:, cols] = in_ref[x, 0, h * HALF : (h + 1) * HALF]


def unpack_kv_kernel(in_ref, keys_ref, values_ref):
    for g in range(8):
        cols = slice(g * HEAD_DIM, (g + 1) * HEAD_DIM)
        y, x = g // 2, 2 * (g % 2)
        for c, out_ref in ((0, keys_ref), (1, values_ref)):
            total = in_ref[x, c, y].astype(jnp.float32) + in_ref[x + 1, c, y].astype(jnp.float32)
            out_ref[:, cols] = total.astype(jnp.bfloat16)


PIECES = ((0, SLAB), (SLAB, SLAB), (2 * SLAB, SLAB // 2), (2 * SLAB + SLAB // 2, SLAB // 2), (3 * SLAB, SLAB))


def main_kernel(where_ref, plan_ref, bounds_ref, packed_ref, lse_ref, delta_ref, *rest):
    mine = rest[0:5]
    other = rest[5:10]
    dq_ref = rest[10]
    keep = rest[11:16]
    send = rest[16:21]
    key_ref, value_ref, dk_ref, dv_ref, dq_sum, slot_ref, sems = rest[21:]
    z, c = where_ref[0], where_ref[1]
    factor = HEAD_DIM ** (-0.5)

    def fetch(first, second):
        copies = []
        for i, (start, size) in enumerate(PIECES):
            rows = pl.ds(start, size)
            copies.append(pltpu.make_async_copy(mine[i], first.at[rows], sems.at[i]))
            copies.append(pltpu.make_async_copy(other[i], second.at[rows], sems.at[5 + i]))
        for copy in copies:
            copy.start()
        return copies

    def fetch_all(first, second):
        copies = fetch(first, second)
        for copy in copies:
            copy.wait()

    dk_ref[...] = jnp.zeros_like(dk_ref)
    dv_ref[...] = jnp.zeros_like(dv_ref)

    def note_slot(slot, carry):
        slot_ref[plan_ref[slot]] = slot
        return carry

    lax.fori_loop(0, 64, note_slot, 0)

    @pl.when(c == 0)
    def _():
        fetch_all(key_ref, value_ref)

    @pl.when(c == 1)
    def _():
        fetch_all(value_ref, key_ref)

    lane = lax.broadcasted_iota(jnp.int32, (1, LANES), 1)
    within = (lane // 256) * HALF + lane % HALF
    row = lax.broadcasted_iota(jnp.int32, (SPAN, LANES), 0)

    def first_row(span):
        slot = slot_ref[span]
        slab = lax.rem(lax.shift_right_logical(slot, 4) - z + 4, 4)
        return pl.multiple_of(slab * SLAB + (slot & 15) * SPAN, SPAN)

    def query_span(s, carry):
        span = plan_ref[(z * 4 + lax.shift_right_logical(s, 1)) * 4 + c * 2 + (s & 1)]
        last = span * SPAN + within
        first = jnp.zeros_like(last)
        first_doc = jnp.int32(0)
        for i in range(1, 12):
            bound = bounds_ref[i]
            first = jnp.where(bound <= last, jnp.maximum(first, bound), first)
            first_doc = jnp.where(bound <= span * SPAN, jnp.maximum(first_doc, bound), first_doc)
        begin = lax.shift_right_logical(first_doc, 7)
        count = span - begin + 1
        queries = jnp.concatenate([packed_ref[2 * s, 0:256], packed_ref[2 * s + 1, 0:256]], axis=0)
        grads = jnp.concatenate([packed_ref[2 * s, 256:512], packed_ref[2 * s + 1, 256:512]], axis=0)
        lse = lse_ref[pl.ds(s, 1), :]
        delta = delta_ref[pl.ds(s, 1), :]
        dq_sum[...] = jnp.zeros_like(dq_sum)

        def pair(i, carry):
            span_a = begin + 2 * i
            has_b = span_a < span
            span_b = jnp.where(has_b, span_a + 1, span_a)
            base_a = span_a * SPAN
            base_b = jnp.where(has_b, span_b * SPAN, 8192)
            row_a = first_row(span_a)
            row_b = first_row(span_b)
            key = jnp.concatenate([key_ref[pl.ds(row_a, SPAN), :], key_ref[pl.ds(row_b, SPAN), :]], axis=0)
            value = jnp.concatenate([value_ref[pl.ds(row_a, SPAN), :], value_ref[pl.ds(row_b, SPAN), :]], axis=0)
            allowed = jnp.concatenate(
                [
                    (row >= first - base_a) & (row <= last - base_a),
                    (row >= first - base_b) & (row <= last - base_b),
                ],
                axis=0,
            )
            scores = dot(key, queries, 1, 1)
            probs = jnp.where(allowed, jnp.exp(scores * factor - lse), 0.0)
            dprob = dot(value, grads, 1, 1)
            dscore = (probs * (dprob - delta)).astype(jnp.bfloat16)
            part_v = dot(probs.astype(jnp.bfloat16), grads, 1, 0)
            part_k = dot(dscore, queries, 1, 0)
            dq_sum[...] += dot(dscore, key, 0, 0)
            dk_ref[pl.ds(row_a, SPAN), :] += part_k[:SPAN]
            dv_ref[pl.ds(row_a, SPAN), :] += part_v[:SPAN]
            dk_ref[pl.ds(row_b, SPAN), :] += part_k[SPAN:]
            dv_ref[pl.ds(row_b, SPAN), :] += part_v[SPAN:]
            return carry

        lax.fori_loop(0, lax.shift_right_logical(count + 1, 1), pair, 0)
        dq = (dq_sum[...] * factor).astype(jnp.bfloat16)
        dq_ref[2 * s] = dq[:256]
        dq_ref[2 * s + 1] = dq[256:]
        return carry

    lax.fori_loop(0, 8, query_span, 0)

    def write(key_outs, value_outs):
        for i, (start, size) in enumerate(PIECES):
            for j in range(0, size, 512):
                rows = slice(start + j, start + j + 512)
                key_outs[i][j : j + 512] = (dk_ref[rows] * factor).astype(jnp.bfloat16)
                value_outs[i][j : j + 512] = dv_ref[rows].astype(jnp.bfloat16)

    @pl.when(c == 0)
    def _():
        write(keep, send)

    @pl.when(c == 1)
    def _():
        write(send, keep)


def shift(array, axis, by):
    return lax.ppermute(array, axis, [(i, (i + by) % 4) for i in range(4)])


def swap(array):
    return lax.ppermute(array, "c", [(0, 1), (1, 0)])


def exchange(array, axes):
    return lax.all_to_all(array, axes, 0, 0, tiled=True)


def shards(queries, keys, values, fwd_out, out_grad, log_norm, doc_bounds, span_plan, read_lists):
    bf16 = jnp.bfloat16
    vmem = pl.BlockSpec(memory_space=pltpu.VMEM)
    smem = pl.BlockSpec(memory_space=pltpu.SMEM)
    anywhere = pl.BlockSpec(memory_space=pl.ANY)
    z, x, c = lax.axis_index("z"), lax.axis_index("x"), lax.axis_index("c")

    kv_out = pl.pallas_call(
        pack_kv_kernel,
        out_shape=jax.ShapeDtypeStruct((4, 2, 4, HALF, HEAD_DIM), bf16),
        in_specs=[vmem, vmem],
        out_specs=vmem,
        name="pack_kv",
    )(keys, values)
    block = exchange(kv_out.reshape(32, HALF, HEAD_DIM), ("x", "c", "y")).reshape(SLAB, HEAD_DIM)

    wide = pl.BlockSpec((HALF, 16 * HEAD_DIM), lambda y: (0, y))
    q_out = pl.pallas_call(
        pack_q_kernel,
        grid=(4,),
        out_shape=jax.ShapeDtypeStruct((4, 4, PACKED, HEAD_DIM), bf16),
        in_specs=[wide, wide, wide],
        out_specs=pl.BlockSpec((4, 1, PACKED, HEAD_DIM), lambda y: (0, y, 0, 0)),
        name="pack_q",
    )(queries, out_grad, fwd_out)
    packed = exchange(q_out.reshape(16, PACKED, HEAD_DIM), ("x", "y"))

    all_lse = lax.all_gather(log_norm.T, "x", axis=0, tiled=False)
    lse = lax.dynamic_slice_in_dim(all_lse, x * 4, 4, 1)
    lse = lse.reshape(4, 4, 2, 2, HALF).transpose(0, 2, 3, 1, 4).reshape(8, LANES)

    from_next = shift(block, "z", -1)
    from_last = shift(block, "z", 1)
    far_a = shift(from_next[: SLAB // 2], "z", -1)
    far_b = shift(from_last[SLAB // 2 :], "z", 1)
    mine = [block, from_next, far_a, far_b, from_last]
    other = [swap(part) for part in mine]

    delta = packed[:, 512:516, :HALF].astype(jnp.float32) + packed[:, 512:516, HALF:].astype(jnp.float32)
    delta = delta.reshape(8, LANES)

    where = jnp.stack([z, c]).astype(jnp.int32)
    pieces = [jax.ShapeDtypeStruct((size, HEAD_DIM), bf16) for _, size in PIECES]
    outs = pl.pallas_call(
        main_kernel,
        out_shape=[jax.ShapeDtypeStruct((16, 256, HEAD_DIM), bf16)] + pieces + pieces,
        in_specs=[smem, smem, smem, vmem, vmem, vmem] + [anywhere] * 10,
        out_specs=[vmem] * 11,
        scratch_shapes=[
            pltpu.VMEM((4 * SLAB, HEAD_DIM), bf16),
            pltpu.VMEM((4 * SLAB, HEAD_DIM), bf16),
            pltpu.VMEM((4 * SLAB, HEAD_DIM), jnp.float32),
            pltpu.VMEM((4 * SLAB, HEAD_DIM), jnp.float32),
            pltpu.VMEM((LANES, HEAD_DIM), jnp.float32),
            pltpu.SMEM((64,), jnp.int32),
            pltpu.SemaphoreType.DMA((10,)),
        ],
        compiler_params=pltpu.CompilerParams(vmem_limit_bytes=48 * MIB),
        name="tiles",
    )(where, span_plan.reshape(-1), doc_bounds, packed, lse, delta, *mine, *other)
    dq, keep, send = outs[0], outs[1:6], outs[6:11]

    dq_back = exchange(dq, ("x", "y")).reshape(4, 4, 256, HEAD_DIM)
    grad_queries = pl.pallas_call(
        unpack_q_kernel,
        grid=(4,),
        out_shape=jax.ShapeDtypeStruct((HALF, 64 * HEAD_DIM), bf16),
        in_specs=[pl.BlockSpec((4, 1, 256, HEAD_DIM), lambda y: (0, y, 0, 0))],
        out_specs=wide,
        name="unpack_q",
    )(dq_back)

    f32 = jnp.float32
    got = [swap(part) for part in send]
    far_a = (keep[2].astype(f32) + got[2].astype(f32)).astype(bf16)
    far_b = (keep[3].astype(f32) + got[3].astype(f32)).astype(bf16)
    via_next = shift(far_a, "z", 1)
    via_last = shift(far_b, "z", -1)
    half = SLAB // 2
    to_next = keep[1].astype(f32) + got[1].astype(f32)
    to_next = jnp.concatenate([to_next[:half] + via_next.astype(f32), to_next[half:]], axis=0).astype(bf16)
    to_last = keep[4].astype(f32) + got[4].astype(f32)
    to_last = jnp.concatenate([to_last[:half], to_last[half:] + via_last.astype(f32)], axis=0).astype(bf16)
    near = shift(to_next, "z", 1).astype(f32) + shift(to_last, "z", -1).astype(f32)
    total = (keep[0].astype(f32) + got[0].astype(f32) + near).astype(bf16)
    kv_back = exchange(total.reshape(32, HALF, HEAD_DIM), ("x", "c", "y"))
    grad_keys, grad_values = pl.pallas_call(
        unpack_kv_kernel,
        out_shape=[jax.ShapeDtypeStruct((HALF, 8 * HEAD_DIM), bf16)] * 2,
        in_specs=[vmem],
        out_specs=[vmem, vmem],
        name="unpack_kv",
    )(kv_back.reshape(4, 2, 4, HALF, HEAD_DIM))
    return (grad_queries, grad_keys, grad_values)


def solution(mesh):
    fine = Mesh(mesh.devices.reshape(4, 4, 2, 4), ROWS)
    rows = P(ROWS, None)
    cp = ("z", "x", "c")
    in_specs = (rows, rows, rows, rows, rows, P(cp, "y"), P(), P(), P(cp, None, None))
    return jax.shard_map(shards, mesh=fine, in_specs=in_specs, out_specs=(rows, rows, rows), check_vma=False)
```

```python
import jax
import jax.numpy as jnp
from jax import lax
from jax.experimental import pallas as pl
from jax.experimental.pallas import tpu as pltpu
from jax.sharding import Mesh, PartitionSpec as P

HEAD_DIM = 128
SPAN = 128
HALF = 64
LANES = 512
PACKED = 528
ROWS = ("z", "x", "c", "y")
MIB = 1024 * 1024


def dot(a, b, ca, cb):
    return lax.dot_general(a, b, (((ca,), (cb,)), ((), ())), preferred_element_type=jnp.float32)


def pack_kv_kernel(keys_ref, values_ref, out_ref):
    for z in range(4):
        for y in range(4):
            cols = slice((2 * y + z // 2) * HEAD_DIM, (2 * y + z // 2 + 1) * HEAD_DIM)
            out_ref[z, y, 0] = keys_ref[:, cols]
            out_ref[z, y, 1] = values_ref[:, cols]


def pack_q_kernel(queries_ref, grad_ref, fwd_ref, out_ref):
    row = lax.broadcasted_iota(jnp.int32, (16, HEAD_DIM), 0)
    for z in range(4):
        delta = jnp.zeros((16, HEAD_DIM), jnp.float32)
        for pair in range(2):
            products = []
            for h in (2 * pair, 2 * pair + 1):
                cols = slice((z * 4 + h) * HEAD_DIM, (z * 4 + h + 1) * HEAD_DIM)
                grad = grad_ref[:, cols]
                out_ref[z, 0, h * HALF : (h + 1) * HALF] = queries_ref[:, cols]
                out_ref[z, 0, 256 + h * HALF : 256 + (h + 1) * HALF] = grad
                products.append(grad.astype(jnp.float32) * fwd_ref[:, cols].astype(jnp.float32))
            product = jnp.concatenate(products, axis=0)
            high = product.astype(jnp.bfloat16)
            low = (product - high.astype(jnp.float32)).astype(jnp.bfloat16)
            pick = ((row == pair) | (row == pair + 2)).astype(jnp.bfloat16)
            delta = delta + dot(pick, high, 1, 1) + dot(pick, low, 1, 1)
        high = delta.astype(jnp.bfloat16).astype(jnp.float32)
        out_ref[z, 0, 512:PACKED] = jnp.where(row < 2, high, delta - high).astype(jnp.bfloat16)


def unpack_q_kernel(in_ref, out_ref):
    for z in range(4):
        for h in range(4):
            cols = slice((z * 4 + h) * HEAD_DIM, (z * 4 + h + 1) * HEAD_DIM)
            out_ref[:, cols] = in_ref[z, 0, h * HALF : (h + 1) * HALF]


def unpack_kv_kernel(in_ref, keys_ref, values_ref):
    for g in range(8):
        cols = slice(g * HEAD_DIM, (g + 1) * HEAD_DIM)
        y, z = g // 2, 2 * (g % 2)
        for i, out_ref in ((0, keys_ref), (1, values_ref)):
            total = in_ref[z, y, i].astype(jnp.float32) + in_ref[z + 1, y, i].astype(jnp.float32)
            out_ref[:, cols] = total.astype(jnp.bfloat16)


PIECES = ((0, 0, 16), (1, 0, 16), (2, 0, 8), (2, 8, 8), (3, 0, 16))
GROUP = 2
MOST = 72


def tiles_kernel(where_ref, plan_ref, bounds_ref, packed_ref, lse_ref, *rest):
    mine, other, dq_ref, keep, send, rest = rest[:5], rest[5:10], rest[10], rest[11:16], rest[16:21], rest[21:]
    kv_ref, dkv_ref, dq_sum, slot_ref, step_ref, base_ref, chunk_ref, lanes_ref, sums_ref, *buffers, sems = rest
    z, x, c = where_ref[0], where_ref[1], where_ref[2]
    factor = HEAD_DIM ** (-0.5)

    copies = []
    for i, (slab, chunk, chunks) in enumerate(PIECES):
        for core, sources in enumerate((mine, other)):
            rows = pl.ds(slab * 32 + core * 16 + chunk, chunks)
            copies.append(pltpu.make_async_copy(sources[i], kv_ref.at[rows], sems.at[2 * i + core]))
    for copy in copies:
        copy.start()

    def note_slot(slot, carry):
        slot_ref[plan_ref[slot]] = slot
        return carry

    lax.fori_loop(0, 64, note_slot, 0)
    dkv_ref[...] = jnp.zeros_like(dkv_ref)
    dq_sum[...] = jnp.zeros_like(dq_sum)
    for buffer in buffers[2:]:
        buffer[...] = jnp.zeros_like(buffer)

    lane = lax.broadcasted_iota(jnp.int32, (1, LANES), 1)
    within = (lane // 256) * HALF + lane % HALF
    row = lax.broadcasted_iota(jnp.int32, (SPAN, LANES), 0)

    steps = jnp.int32(0)
    for s in range(8):
        span = plan_ref[(s // 2) * 16 + x * 4 + c * 2 + s % 2]
        last = span * SPAN + within
        first = jnp.zeros_like(last)
        first_doc = jnp.int32(0)
        for i in range(1, 12):
            bound = bounds_ref[i]
            first = jnp.where(bound <= last, jnp.maximum(first, bound), first)
            first_doc = jnp.where(bound <= span * SPAN, jnp.maximum(first_doc, bound), first_doc)
        lanes_ref[s, 0:1] = first
        lanes_ref[s, 1:2] = last
        parts = [packed_ref[2 * s + i, 512:PACKED].astype(jnp.float32) for i in range(2)]
        sums_ref[s, 0:1] = lse_ref[pl.ds(((s // 2 - z) & 3) * 2 + s % 2, 1), :]
        sums_ref[s, 1:2] = jnp.concatenate(
            [part[h : h + 1] + part[h + 2 : h + 3] for part in parts for h in range(2)], axis=1
        )

        def note_span(i, carry, s=s, begin=lax.shift_right_logical(first_doc, 7), span=span, steps=steps):
            key_span = jnp.minimum(begin + i, span)
            slot = slot_ref[key_span]
            slab = (lax.shift_right_logical(slot, 2) - x) & 3
            core = (lax.shift_right_logical(slot, 1) & 1) ^ c
            step_ref[steps + lax.shift_right_logical(i, 1)] = s
            base_ref[2 * steps + i] = jnp.where(begin + i <= span, key_span * SPAN, 8192)
            chunk_ref[2 * steps + i] = (
                slab * 32 + core * 16 + lax.shift_right_logical(slot, 4) * 4 + (slot & 1) * 2
            )
            return carry

        pairs = lax.shift_right_logical(span - lax.shift_right_logical(first_doc, 7) + 2, 1)
        lax.fori_loop(0, 2 * pairs, note_span, 0)
        steps = steps + pairs
    for i in range(2):
        step_ref[steps + i] = 7
    for i in range(4):
        base_ref[2 * steps + i] = 8192
        chunk_ref[2 * steps + i] = 0
    for copy in copies:
        copy.wait()

    def operand(s, start):
        return jnp.concatenate([packed_ref[2 * s + i, start : start + 256] for i in range(2)], axis=0)

    def tile(step, i):
        chunks = [chunk_ref[2 * step + j] for j in range(GROUP)]
        return jnp.concatenate([kv_ref[pl.ds(r, 2), i].reshape(SPAN, HEAD_DIM) for r in chunks], axis=0)

    def scores_stage(step, probs_ref, dscore_ref):
        s = step_ref[step]
        first, last = lanes_ref[s, 0:1], lanes_ref[s, 1:2]
        lse, delta = sums_ref[s, 0:1], sums_ref[s, 1:2]
        masks = []
        for j in range(GROUP):
            base = base_ref[2 * step + j]
            masks.append((row >= first - base) & (row <= last - base))
        allowed = jnp.concatenate(masks, axis=0)
        scores = dot(tile(step, 0), operand(s, 0), 1, 1)
        probs = jnp.where(allowed, jnp.exp(scores * factor - lse), 0.0)
        dprob = dot(tile(step, 1), operand(s, 256), 1, 1)
        probs_ref[...] = probs.astype(jnp.bfloat16)
        dscore_ref[...] = (probs * (dprob - delta)).astype(jnp.bfloat16)

    def sums_stage(step, probs_ref, dscore_ref):
        s = step_ref[step]
        probs, dscore = probs_ref[...], dscore_ref[...]
        part_v = dot(probs, operand(s, 256), 1, 0)
        part_k = dot(dscore, operand(s, 0), 1, 0)
        dq_sum[s] += dot(tile(step, 0), dscore, 0, 0)
        for i, part in ((0, part_k), (1, part_v)):
            part = part.reshape(2 * GROUP, HALF, HEAD_DIM)
            for j in range(GROUP):
                dkv_ref[pl.ds(chunk_ref[2 * step + j], 2), i] += part[2 * j : 2 * j + 2]

    def two_steps(i, carry):
        step = 2 * i
        scores_stage(step, buffers[0], buffers[1])
        sums_stage(jnp.maximum(step - 1, 0), buffers[2], buffers[3])
        scores_stage(step + 1, buffers[2], buffers[3])
        sums_stage(step, buffers[0], buffers[1])
        return carry

    loops = lax.shift_right_logical(steps + 1, 1)
    lax.fori_loop(0, loops, two_steps, 0)
    sums_stage(jnp.maximum(2 * loops - 1, 0), buffers[2], buffers[3])

    for i in range(16):
        rows = slice((i % 2) * 256, (i % 2) * 256 + 256)
        dq_ref[i] = jnp.transpose(dq_sum[i // 2, :, rows] * factor).astype(jnp.bfloat16)
    for i, (slab, chunk, chunks) in enumerate(PIECES):
        for core, outs in enumerate((keep, send)):
            start = slab * 32 + core * 16 + chunk
            for j in range(0, chunks, 4):
                rows = slice(start + j, start + j + 4)
                outs[i][j : j + 4, 0] = (dkv_ref[rows, 0] * factor).astype(jnp.bfloat16)
                outs[i][j : j + 4, 1] = dkv_ref[rows, 1].astype(jnp.bfloat16)


def tiles(where, plan, bounds, packed, lse, mine, other):
    bf16, f32 = jnp.bfloat16, jnp.float32
    vmem = pl.BlockSpec(memory_space=pltpu.VMEM)
    smem = pl.BlockSpec(memory_space=pltpu.SMEM)
    anywhere = pl.BlockSpec(memory_space=pl.ANY)
    parts = [jax.ShapeDtypeStruct((chunks, 2, HALF, HEAD_DIM), bf16) for _, _, chunks in PIECES]
    outs = pl.pallas_call(
        tiles_kernel,
        out_shape=[jax.ShapeDtypeStruct((16, 256, HEAD_DIM), bf16)] + parts + parts,
        in_specs=[smem, smem, smem, vmem, vmem] + [anywhere] * 10,
        out_specs=[vmem] * 11,
        scratch_shapes=[
            pltpu.VMEM((128, 2, HALF, HEAD_DIM), bf16),
            pltpu.VMEM((128, 2, HALF, HEAD_DIM), f32),
            pltpu.VMEM((8, HEAD_DIM, LANES), f32),
            pltpu.SMEM((64,), jnp.int32),
            pltpu.SMEM((MOST,), jnp.int32),
            pltpu.SMEM((2 * MOST,), jnp.int32),
            pltpu.SMEM((2 * MOST,), jnp.int32),
            pltpu.VMEM((8, 2, LANES), jnp.int32),
            pltpu.VMEM((8, 2, LANES), f32),
        ]
        + [pltpu.VMEM((GROUP * SPAN, LANES), bf16)] * 4
        + [pltpu.SemaphoreType.DMA((10,))],
        compiler_params=pltpu.CompilerParams(vmem_limit_bytes=26 * MIB),
        name="tiles",
    )(where, plan, bounds, packed, lse, *mine, *other)
    return outs[0], outs[1:6], outs[6:11]


def shift(array, axis, by):
    return lax.ppermute(array, axis, [(i, (i + by) % 4) for i in range(4)])


def swap(array):
    return lax.ppermute(array, "c", [(0, 1), (1, 0)])


def exchange(array):
    return lax.all_to_all(array, ("z", "y"), 0, 0, tiled=True)


def shards(queries, keys, values, fwd_out, out_grad, log_norm, doc_bounds, span_plan, read_lists):
    bf16 = jnp.bfloat16
    f32 = jnp.float32
    vmem = pl.BlockSpec(memory_space=pltpu.VMEM)
    z, x = lax.axis_index("z"), lax.axis_index("x")
    c = lax.axis_index("c")

    kv_out = pl.pallas_call(
        pack_kv_kernel,
        out_shape=jax.ShapeDtypeStruct((4, 4, 2, HALF, HEAD_DIM), bf16),
        in_specs=[vmem, vmem],
        out_specs=vmem,
        name="pack_kv",
    )(keys, values)
    block = exchange(kv_out.reshape(16, 2, HALF, HEAD_DIM))

    wide = pl.BlockSpec((HALF, 16 * HEAD_DIM), lambda y: (0, y))
    q_out = pl.pallas_call(
        pack_q_kernel,
        grid=(4,),
        out_shape=jax.ShapeDtypeStruct((4, 4, PACKED, HEAD_DIM), bf16),
        in_specs=[wide, wide, wide],
        out_specs=pl.BlockSpec((4, 1, PACKED, HEAD_DIM), lambda y: (0, y, 0, 0)),
        name="pack_q",
    )(queries, out_grad, fwd_out)
    norms = log_norm.reshape(2, 2, HALF, 4, 4).transpose(3, 0, 1, 4, 2).reshape(4, 2, LANES)
    to = [lax.dynamic_index_in_dim(norms, (z + k) % 4, 0, keepdims=False) for k in range(4)]
    lse = jnp.concatenate(
        [to[0], shift(to[3], "z", -1), shift(to[2], "z", 2), shift(to[1], "z", 1)], axis=0
    )
    q_out, lse = lax.optimization_barrier((q_out, lse))
    packed = exchange(q_out.reshape(16, PACKED, HEAD_DIM))

    from_next = shift(block, "x", -1)
    from_last = shift(block, "x", 1)
    far_a = shift(from_next[:8], "x", -1)
    far_b = shift(from_last[8:], "x", 1)

    where = jnp.stack([z, x, c]).astype(jnp.int32)
    mine = [block, from_next, far_a, far_b, from_last]
    other = [swap(part) for part in mine]
    dq, keep, send = tiles(where, span_plan.reshape(-1), doc_bounds, packed, lse, mine, other)

    got = [swap(part) for part in send]
    sums = [a.astype(f32) + b.astype(f32) for a, b in zip(keep, got)]
    via_next = shift(sums[2].astype(bf16), "x", 1).astype(f32)
    via_last = shift(sums[3].astype(bf16), "x", -1).astype(f32)
    to_next = jnp.concatenate([sums[1][:8] + via_next, sums[1][8:]], axis=0).astype(bf16)
    to_last = jnp.concatenate([sums[4][:8], sums[4][8:] + via_last], axis=0).astype(bf16)
    dq, sums[1], sums[4] = lax.optimization_barrier((dq, sums[1], sums[4]))
    dq_back = exchange(dq).reshape(4, 4, 256, HEAD_DIM)
    grad_queries = pl.pallas_call(
        unpack_q_kernel,
        grid=(4,),
        out_shape=jax.ShapeDtypeStruct((HALF, 64 * HEAD_DIM), bf16),
        in_specs=[pl.BlockSpec((4, 1, 256, HEAD_DIM), lambda y: (0, y, 0, 0))],
        out_specs=wide,
        compiler_params=pltpu.CompilerParams(vmem_limit_bytes=6 * MIB),
        name="unpack_q",
    )(dq_back)

    near = shift(to_next, "x", 1).astype(f32) + shift(to_last, "x", -1).astype(f32)
    kv_back = exchange((sums[0] + near).astype(bf16))
    grad_keys, grad_values = pl.pallas_call(
        unpack_kv_kernel,
        out_shape=[jax.ShapeDtypeStruct((HALF, 8 * HEAD_DIM), bf16)] * 2,
        in_specs=[vmem],
        out_specs=[vmem, vmem],
        compiler_params=pltpu.CompilerParams(vmem_limit_bytes=4 * MIB),
        name="unpack_kv",
    )(kv_back.reshape(4, 4, 2, HALF, HEAD_DIM))
    return (grad_queries, grad_keys, grad_values)


def solution(mesh):
    fine = Mesh(mesh.devices.reshape(4, 4, 2, 4), ROWS)
    rows = P(ROWS, None)
    cp = ("z", "x", "c")
    in_specs = (rows, rows, rows, rows, rows, P(cp, "y"), P(), P(), P(cp, None, None))
    return jax.shard_map(shards, mesh=fine, in_specs=in_specs, out_specs=(rows, rows, rows), check_vma=False)
```

```python
import functools

import jax
import jax.numpy as jnp
from jax import lax
from jax.experimental import pallas as pl
from jax.experimental.pallas import tpu as pltpu
from jax.sharding import Mesh, PartitionSpec as P

HEAD_DIM = 128
SPAN = 128
HALF = 64
LANES = 512
PACKED = 272
ROWS = ("z", "x", "c", "y")
MIB = 1024 * 1024


def dot(a, b, ca, cb):
    return lax.dot_general(a, b, (((ca,), (cb,)), ((), ())), preferred_element_type=jnp.float32)


def pack_kv_kernel(keys_ref, values_ref, out_ref):
    for z in range(4):
        for y in range(4):
            cols = slice((2 * y + z // 2) * HEAD_DIM, (2 * y + z // 2 + 1) * HEAD_DIM)
            out_ref[z, y, 0] = keys_ref[:, cols]
            out_ref[z, y, 1] = values_ref[:, cols]


def pack_q_kernel(queries_ref, grad_ref, fwd_ref, out_ref):
    row = lax.broadcasted_iota(jnp.int32, (16, HEAD_DIM), 0)
    pick = (row < 2).astype(jnp.bfloat16)
    for z in range(4):
        for pair in range(2):
            cols = [slice((z * 4 + 2 * pair + i) * HEAD_DIM, (z * 4 + 2 * pair + i + 1) * HEAD_DIM) for i in range(2)]
            lanes = slice(pair * HEAD_DIM, (pair + 1) * HEAD_DIM)
            query = jnp.concatenate([queries_ref[:, col] for col in cols], axis=0)
            grad = jnp.concatenate([grad_ref[:, col] for col in cols], axis=0)
            fwd = jnp.concatenate([fwd_ref[:, col] for col in cols], axis=0)
            out_ref[z, 0, 0:HEAD_DIM, lanes] = jnp.transpose(query)
            out_ref[z, 0, HEAD_DIM : 2 * HEAD_DIM, lanes] = jnp.transpose(grad)
            product = grad.astype(jnp.float32) * fwd.astype(jnp.float32)
            high = product.astype(jnp.bfloat16)
            low = (product - high.astype(jnp.float32)).astype(jnp.bfloat16)
            delta = dot(pick, high, 1, 1) + dot(pick, low, 1, 1)
            high = delta.astype(jnp.bfloat16).astype(jnp.float32)
            out_ref[z, 0, 2 * HEAD_DIM : PACKED, lanes] = jnp.where(row < 1, high, delta - high).astype(jnp.bfloat16)


def unpack_q_kernel(in_ref, out_ref):
    for z in range(4):
        for pair in range(2):
            part = jnp.transpose(in_ref[z, 0, :, pair * HEAD_DIM : (pair + 1) * HEAD_DIM])
            for i in range(2):
                head = z * 4 + 2 * pair + i
                out_ref[:, head * HEAD_DIM : (head + 1) * HEAD_DIM] = part[i * HALF : (i + 1) * HALF]


def add_kernel(terms, *refs):
    count = len(refs) // (terms + 1)
    for i in range(count):
        for t in range(4):
            total = refs[i * terms][t].astype(jnp.float32)
            for k in range(1, terms):
                total = total + refs[i * terms + k][t].astype(jnp.float32)
            refs[count * terms + i][t] = total.astype(jnp.bfloat16)


def final_kernel(keep_ref, got_ref, last_a_ref, last_b_ref, next_a_ref, next_b_ref, out_ref):
    for t in range(8):
        last_ref, next_ref = ((last_a_ref, next_a_ref), (last_b_ref, next_b_ref))[t // 4]
        for i in range(2):
            total = keep_ref[t, i].astype(jnp.float32) + got_ref[t, i].astype(jnp.float32)
            total = total + last_ref[t % 4, i].astype(jnp.float32) + next_ref[t % 4, i].astype(jnp.float32)
            rows = jnp.transpose(total).astype(jnp.bfloat16)
            out_ref[2 * t, i] = rows[:HALF]
            out_ref[2 * t + 1, i] = rows[HALF:]


def unpack_kv_kernel(in_ref, keys_ref, values_ref):
    for g in range(8):
        cols = slice(g * HEAD_DIM, (g + 1) * HEAD_DIM)
        y, z = g // 2, 2 * (g % 2)
        for i, out_ref in ((0, keys_ref), (1, values_ref)):
            total = in_ref[z, y, i].astype(jnp.float32) + in_ref[z + 1, y, i].astype(jnp.float32)
            out_ref[:, cols] = total.astype(jnp.bfloat16)


PIECES = ((0, 0, 8), (1, 0, 8), (2, 0, 4), (2, 4, 4), (3, 0, 8))
GROUP = 2
QUERY, BEGIN, TABLE = 64, 72, 80


def tiles_kernel(plan_in, bounds_in, packed_ref, lse_ref, *rest):
    mine, other, dq_ref, keep, send, rest = rest[:5], rest[5:10], rest[10], rest[11:15], rest[15:19], rest[19:]
    plan_ref, bounds_ref, table_ref, kv_ref, dkv_ref, dq_sum, dq_out, keep_out, lanes_ref, sums_ref, *buffers, sems = rest
    z, x, c = lax.axis_index("z"), lax.axis_index("x"), lax.axis_index("c")
    factor = HEAD_DIM ** (-0.5)

    small = [
        pltpu.make_async_copy(plan_in, plan_ref, sems.at[10]),
        pltpu.make_async_copy(bounds_in, bounds_ref, sems.at[11]),
    ]
    for copy in small:
        copy.start()
    copies = []
    for i, (slab, tile, count) in enumerate(PIECES):
        for core, sources in enumerate((mine, other)):
            rows = pl.ds(slab * 16 + core * 8 + tile, count)
            copies.append(pltpu.make_async_copy(sources[i], kv_ref.at[rows], sems.at[2 * i + core]))
    for copy in copies:
        copy.start()

    dkv_ref[...] = jnp.zeros_like(dkv_ref)
    dq_sum[...] = jnp.zeros_like(dq_sum)
    for buffer in buffers[2:]:
        buffer[...] = jnp.zeros_like(buffer)
    for copy in small:
        copy.wait()
    slabs = [((i - x) & 3) * 16 for i in range(4)]
    cores = [c * 8, (1 - c) * 8]
    for slot in range(64):
        place = slabs[slot // 4 % 4] + cores[slot // 2 % 2] + slot // 16 * 2 + slot % 2
        table_ref[plan_ref[slot // 2, slot % 2]] = place
    row = lax.broadcasted_iota(jnp.int32, (SPAN, LANES), 0)
    lane = lax.broadcasted_iota(jnp.int32, (1, LANES), 1)
    within = (lane // 256) * HALF + lane % HALF
    bounds = [bounds_ref[i] for i in range(1, 12)]
    steps = jnp.int32(0)
    for s in range(8):
        span = plan_ref[(s // 2) * 8 + x * 2 + c, s % 2]
        last = span * SPAN + within
        first = jnp.zeros_like(last)
        first_doc = jnp.int32(0)
        for bound in bounds:
            first = jnp.where(bound <= last, jnp.maximum(first, bound), first)
            first_doc = jnp.where(bound <= span * SPAN, jnp.maximum(first_doc, bound), first_doc)
        begin = lax.shift_right_logical(first_doc, 7)
        table_ref[QUERY + s] = span
        table_ref[BEGIN + s] = begin
        steps = steps + lax.shift_right_logical(span - begin + GROUP, 1)
        lanes_ref[s, 0:1] = first
        lanes_ref[s, 1:2] = last
        sums_ref[s, 0:1] = lse_ref[pl.ds(((s // 2 - z) & 3) * 2 + s % 2, 1), :]
        parts = [packed_ref[2 * s + i, 2 * HEAD_DIM : PACKED].astype(jnp.float32) for i in range(2)]
        sums_ref[s, 1:2] = jnp.concatenate([part[0:1] + part[1:2] for part in parts], axis=1)
    for copy in copies:
        copy.wait()

    def operand(s, start):
        return jnp.concatenate([packed_ref[2 * s + i, start : start + HEAD_DIM] for i in range(2)], axis=1)

    def tiles_of(item):
        s, span = item
        return [table_ref[jnp.minimum(span + j, table_ref[QUERY + s])] for j in range(GROUP)]

    def tile(item, i):
        return jnp.concatenate([kv_ref[t, :, i].reshape(SPAN, HEAD_DIM) for t in tiles_of(item)], axis=0)

    def scores_stage(item, live, probs_ref, dscore_ref):
        s, span = item
        first, last = lanes_ref[s, 0:1], lanes_ref[s, 1:2]
        lse, delta = sums_ref[s, 0:1], sums_ref[s, 1:2]
        masks = []
        for j in range(GROUP):
            base = jnp.where(live & (span + j <= table_ref[QUERY + s]), (span + j) * SPAN, 8192)
            masks.append((row >= first - base) & (row <= last - base))
        allowed = jnp.concatenate(masks, axis=0)
        scores = dot(tile(item, 0), operand(s, 0), 1, 0)
        probs = jnp.where(allowed, jnp.exp(scores * factor - lse), 0.0)
        dprob = dot(tile(item, 1), operand(s, HEAD_DIM), 1, 0)
        probs_ref[...] = probs.astype(jnp.bfloat16)
        dscore_ref[...] = (probs * (dprob - delta)).astype(jnp.bfloat16)

    def sums_stage(item, probs_ref, dscore_ref):
        s, span = item
        probs, dscore = probs_ref[...], dscore_ref[...]
        part_v = dot(operand(s, HEAD_DIM), probs, 1, 1)
        part_k = dot(operand(s, 0), dscore, 1, 1)
        dq_sum[s] += dot(tile(item, 0), dscore, 0, 0)
        for i, part in ((0, part_k), (1, part_v)):
            for j, t in enumerate(tiles_of(item)):
                dkv_ref[t, i] += part[:, j * SPAN : (j + 1) * SPAN]

    def advance(item):
        s, span = item
        done = span + GROUP > table_ref[QUERY + s]
        following = jnp.where(done, jnp.minimum(s + 1, 7), s)
        return following, jnp.where(done, table_ref[BEGIN + following], span + GROUP)

    def two_steps(i, carry):
        before, item = carry
        scores_stage(item, True, buffers[0], buffers[1])
        sums_stage(before, buffers[2], buffers[3])
        following = advance(item)
        scores_stage(following, 2 * i + 1 < steps, buffers[2], buffers[3])
        sums_stage(item, buffers[0], buffers[1])
        return following, advance(following)

    start = (jnp.int32(0), table_ref[BEGIN])
    final, _ = lax.fori_loop(0, lax.shift_right_logical(steps + 1, 1), two_steps, (start, start))
    sums_stage(final, buffers[2], buffers[3])

    leaving = []

    def leave(source, target, sem):
        leaving.append(pltpu.make_async_copy(source, target, sem))
        leaving[-1].start()

    for i in range(16):
        lanes = slice((i % 2) * 256, (i % 2) * 256 + 256)
        dq_out[i] = (dq_sum[i // 2, :, lanes] * factor).astype(jnp.bfloat16)
    leave(dq_out, dq_ref, sems.at[12])
    for core in range(2):
        for slab in (2, 1, 3, 0):
            for t in range(8):
                start = slab * 16 + core * 8 + t
                key = (dkv_ref[start, 0] * factor).astype(jnp.bfloat16)
                value = dkv_ref[start, 1].astype(jnp.bfloat16)
                if core == 0:
                    keep_out[slab, t, 0], keep_out[slab, t, 1] = key, value
                else:
                    send[slab][t, 0], send[slab][t, 1] = key, value
            if core == 0:
                leave(keep_out.at[slab], keep[slab], sems.at[13 + slab])
    for copy in leaving:
        copy.wait()


VMEM = pl.BlockSpec(memory_space=pltpu.VMEM)
HBM = pl.BlockSpec(memory_space=pltpu.HBM)


def tiles(plan, bounds, packed, lse, mine, other):
    bf16, f32 = jnp.bfloat16, jnp.float32
    parts = [jax.ShapeDtypeStruct((8, 2, HEAD_DIM, SPAN), bf16)] * 4
    outs = pl.pallas_call(
        tiles_kernel,
        out_shape=[pltpu.HBM((16, HEAD_DIM, 256), bf16)] + [pltpu.HBM((8, 2, HEAD_DIM, SPAN), bf16)] * 4 + parts,
        in_specs=[HBM] * 2 + [VMEM] * 2 + [pl.BlockSpec(memory_space=pl.ANY)] * 10,
        out_specs=[HBM] * 5 + [VMEM] * 4,
        scratch_shapes=[
            pltpu.SMEM((32, 2), jnp.int32),
            pltpu.SMEM((12,), jnp.int32),
            pltpu.SMEM((TABLE,), jnp.int32),
            pltpu.VMEM((64, 2, 2, HALF, HEAD_DIM), bf16),
            pltpu.VMEM((64, 2, HEAD_DIM, SPAN), f32),
            pltpu.VMEM((8, HEAD_DIM, LANES), f32),
            pltpu.VMEM((16, HEAD_DIM, 256), bf16),
            pltpu.VMEM((4, 8, 2, HEAD_DIM, SPAN), bf16),
            pltpu.VMEM((8, 2, LANES), jnp.int32),
            pltpu.VMEM((8, 2, LANES), f32),
        ]
        + [pltpu.VMEM((GROUP * SPAN, LANES), bf16)] * 4
        + [pltpu.SemaphoreType.DMA((17,))],
        compiler_params=pltpu.CompilerParams(vmem_limit_bytes=26 * MIB),
        name="tiles",
    )(plan, bounds, packed, lse, *[part.reshape(-1, 2, 2, HALF, HEAD_DIM) for part in (*mine, *other)])
    return outs[0], outs[1:5], outs[5:9]


def shift(array, axis, by):
    return lax.ppermute(array, axis, [(i, (i + by) % 4) for i in range(4)])


def in_hbm(array):
    return pltpu.with_memory_space_constraint(array, pltpu.HBM)


def swap(array):
    return lax.ppermute(array, "c", [(0, 1), (1, 0)])


def exchange(array):
    return lax.all_to_all(array, ("z", "y"), 0, 0, tiled=True)


def shards(queries, keys, values, fwd_out, out_grad, log_norm, doc_bounds, span_plan, read_lists):
    bf16 = jnp.bfloat16
    f32 = jnp.float32
    z = lax.axis_index("z")

    kv_out = pl.pallas_call(
        pack_kv_kernel,
        out_shape=jax.ShapeDtypeStruct((4, 4, 2, HALF, HEAD_DIM), bf16),
        in_specs=[VMEM, VMEM],
        out_specs=VMEM,
        name="pack_kv",
    )(keys, values)
    block = exchange(kv_out.reshape(16, 2, HALF, HEAD_DIM))

    wide = pl.BlockSpec((HALF, 16 * HEAD_DIM), lambda y: (0, y))
    q_out = pl.pallas_call(
        pack_q_kernel,
        grid=(4,),
        out_shape=jax.ShapeDtypeStruct((4, 4, PACKED, 256), bf16),
        in_specs=[wide, wide, wide],
        out_specs=pl.BlockSpec((4, 1, PACKED, 256), lambda y: (0, y, 0, 0)),
        name="pack_q",
    )(queries, out_grad, fwd_out)
    norms = log_norm.reshape(2, 2, HALF, 4, 4).transpose(3, 0, 1, 4, 2).reshape(4, 2, LANES)
    to = [lax.dynamic_index_in_dim(norms, (z + k) % 4, 0, keepdims=False) for k in range(4)]
    lse = jnp.concatenate(
        [to[0], shift(to[3], "z", -1), shift(to[2], "z", 2), shift(to[1], "z", 1)], axis=0
    )
    q_out, lse = lax.optimization_barrier((q_out, lse))
    packed = exchange(q_out.reshape(16, PACKED, 256))

    from_next = shift(block, "x", -1)
    from_last = shift(block, "x", 1)
    far_a = shift(from_next[:8], "x", -1)
    far_b = shift(from_last[8:], "x", 1)

    plan, bounds = in_hbm(span_plan), in_hbm(doc_bounds)
    mine = [block, from_next, far_a, far_b, from_last]
    other = [swap(part) for part in mine]
    dq, keep, send = tiles(plan, bounds, packed, lse, mine, other)

    got = {k: in_hbm(swap(send[k])) for k in (2, 1, 3, 0)}
    keep = [in_hbm(part) for part in keep]
    half = [pl.BlockSpec((4, 2, HEAD_DIM, SPAN), lambda _, i=i: (i, 0, 0, 0)) for i in range(2)]
    piece = jax.ShapeDtypeStruct((4, 2, HEAD_DIM, SPAN), bf16)
    via_next, via_last, last_b, next_a = pl.pallas_call(
        functools.partial(add_kernel, 2),
        grid=(1,),
        out_shape=[piece] * 4,
        in_specs=[half[0]] * 2 + [half[1]] * 4 + [half[0]] * 2,
        out_specs=[half[0]] * 4,
        compiler_params=pltpu.CompilerParams(vmem_limit_bytes=8 * MIB),
        name="first_sums",
    )(keep[2], got[2], keep[2], got[2], keep[1], got[1], keep[3], got[3])
    via_next, via_last = shift(via_next, "x", 1), shift(via_last, "x", -1)
    last_b, next_a = shift(last_b, "x", 1), shift(next_a, "x", -1)
    last_a, next_b = pl.pallas_call(
        functools.partial(add_kernel, 3),
        grid=(1,),
        out_shape=[piece] * 2,
        in_specs=[half[0]] * 3 + [half[1]] * 2 + [half[0]],
        out_specs=[half[0]] * 2,
        compiler_params=pltpu.CompilerParams(vmem_limit_bytes=6 * MIB),
        name="second_sums",
    )(keep[1], got[1], via_next, keep[3], got[3], via_last)
    last_a, next_b = shift(last_a, "x", 1), shift(next_b, "x", -1)
    dq_back = exchange(dq).reshape(4, 4, HEAD_DIM, 256)
    total = pl.pallas_call(
        final_kernel,
        out_shape=jax.ShapeDtypeStruct((16, 2, HALF, HEAD_DIM), bf16),
        in_specs=[VMEM] * 6,
        out_specs=VMEM,
        compiler_params=pltpu.CompilerParams(vmem_limit_bytes=6 * MIB),
        name="own_slab",
    )(keep[0], got[0], last_a, last_b, next_a, next_b)
    total, dq_back = lax.optimization_barrier((total, dq_back))
    kv_back = exchange(total)
    grad_queries = pl.pallas_call(
        unpack_q_kernel,
        grid=(4,),
        out_shape=jax.ShapeDtypeStruct((HALF, 64 * HEAD_DIM), bf16),
        in_specs=[pl.BlockSpec((4, 1, HEAD_DIM, 256), lambda y: (0, y, 0, 0))],
        out_specs=wide,
        compiler_params=pltpu.CompilerParams(vmem_limit_bytes=6 * MIB),
        name="unpack_q",
    )(dq_back)
    grad_keys, grad_values = pl.pallas_call(
        unpack_kv_kernel,
        out_shape=[jax.ShapeDtypeStruct((HALF, 8 * HEAD_DIM), bf16)] * 2,
        in_specs=[VMEM],
        out_specs=[VMEM, VMEM],
        compiler_params=pltpu.CompilerParams(vmem_limit_bytes=4 * MIB),
        name="unpack_kv",
    )(kv_back.reshape(4, 4, 2, HALF, HEAD_DIM))
    return (grad_queries, grad_keys, grad_values)


def solution(mesh):
    fine = Mesh(mesh.devices.reshape(4, 4, 2, 4), ROWS)
    rows = P(ROWS, None)
    cp = ("z", "x", "c")
    in_specs = (rows, rows, rows, rows, rows, P(cp, "y"), P(), P(), P(cp, None, None))
    return jax.shard_map(shards, mesh=fine, in_specs=in_specs, out_specs=(rows, rows, rows), check_vma=False)
```

```python
import functools

import jax
import jax.numpy as jnp
from jax import lax
from jax.experimental import pallas as pl
from jax.experimental.pallas import tpu as pltpu
from jax.sharding import Mesh, PartitionSpec as P

HEAD_DIM = 128
SPAN = 128
HALF = 64
LOG2E = 1.4426950408889634
LANES = 512
PACKED = 272
ROWS = ("z", "x", "c", "y")
MIB = 1024 * 1024


def dot(a, b, ca, cb):
    return lax.dot_general(a, b, (((ca,), (cb,)), ((), ())), preferred_element_type=jnp.float32)


def pack_kv_kernel(keys_ref, values_ref, out_ref):
    for z in range(4):
        for y in range(4):
            cols = slice((2 * y + z // 2) * HEAD_DIM, (2 * y + z // 2 + 1) * HEAD_DIM)
            out_ref[z, y, 0] = keys_ref[:, cols]
            out_ref[z, y, 1] = values_ref[:, cols]


def pack_q_kernel(queries_ref, grad_ref, fwd_ref, norms_ref, out_ref):
    row = lax.broadcasted_iota(jnp.int32, (16, HEAD_DIM), 0)
    pick = (row < 2).astype(jnp.bfloat16)
    for z in range(4):
        for pair in range(2):
            cols = [slice((z * 4 + 2 * pair + i) * HEAD_DIM, (z * 4 + 2 * pair + i + 1) * HEAD_DIM) for i in range(2)]
            lanes = slice(pair * HEAD_DIM, (pair + 1) * HEAD_DIM)
            query = jnp.concatenate([queries_ref[:, col] for col in cols], axis=0)
            grad = jnp.concatenate([grad_ref[:, col] for col in cols], axis=0)
            fwd = jnp.concatenate([fwd_ref[:, col] for col in cols], axis=0)
            out_ref[z, 0, 0:HEAD_DIM, lanes] = jnp.transpose(query)
            out_ref[z, 0, HEAD_DIM : 2 * HEAD_DIM, lanes] = jnp.transpose(grad)
            product = grad.astype(jnp.float32) * fwd.astype(jnp.float32)
            high = product.astype(jnp.bfloat16)
            low = (product - high.astype(jnp.float32)).astype(jnp.bfloat16)
            delta = dot(pick, high, 1, 1) + dot(pick, low, 1, 1)
            high = delta.astype(jnp.bfloat16).astype(jnp.float32)
            pieces, rest = [], norms_ref[z, :, lanes]
            for _ in range(3):
                pieces.append(rest.astype(jnp.bfloat16).astype(jnp.float32))
                rest = rest - pieces[-1]
            tail = jnp.concatenate([high[0:1], (delta - high)[1:2], *pieces, high[0:2]], axis=0)
            out_ref[z, 0, 2 * HEAD_DIM : PACKED, lanes] = tail.astype(jnp.bfloat16)


def unpack_q_kernel(in_ref, out_ref):
    for z in range(4):
        for pair in range(2):
            part = jnp.transpose(in_ref[z, 0, :, pair * HEAD_DIM : (pair + 1) * HEAD_DIM])
            for i in range(2):
                head = z * 4 + 2 * pair + i
                out_ref[:, head * HEAD_DIM : (head + 1) * HEAD_DIM] = part[i * HALF : (i + 1) * HALF]


def add_kernel(terms, *refs):
    count = len(refs) // (terms + 1)
    for i in range(count):
        for t in range(4):
            total = refs[i * terms][0, t].astype(jnp.float32)
            for k in range(1, terms):
                total = total + refs[i * terms + k][0, t].astype(jnp.float32)
            refs[count * terms + i][0, t] = total.astype(jnp.bfloat16)


def final_kernel(keep_ref, got_ref, last_a_ref, last_b_ref, next_a_ref, next_b_ref, out_ref):
    for t in range(8):
        last_ref, next_ref = ((last_a_ref, next_a_ref), (last_b_ref, next_b_ref))[t // 4]
        for i in range(2):
            total = keep_ref[0, t, i].astype(jnp.float32) + got_ref[0, t, i].astype(jnp.float32)
            total = total + last_ref[0, t % 4, i].astype(jnp.float32) + next_ref[0, t % 4, i].astype(jnp.float32)
            rows = jnp.transpose(total).astype(jnp.bfloat16)
            out_ref[2 * t, i] = rows[:HALF]
            out_ref[2 * t + 1, i] = rows[HALF:]


def unpack_kv_kernel(in_ref, keys_ref, values_ref):
    for g in range(8):
        cols = slice(g * HEAD_DIM, (g + 1) * HEAD_DIM)
        y, z = g // 2, 2 * (g % 2)
        for i, out_ref in ((0, keys_ref), (1, values_ref)):
            total = in_ref[z, y, i].astype(jnp.float32) + in_ref[z + 1, y, i].astype(jnp.float32)
            out_ref[:, cols] = total.astype(jnp.bfloat16)


PIECES = ((0, 0, 8), (1, 0, 8), (2, 0, 4), (2, 4, 4), (3, 0, 8))
GROUP = 2
QUERY, BEGIN, TABLE = 64, 72, 80


def tiles_kernel(plan_in, bounds_in, packed_ref, *rest):
    mine, other, (dq_ref, keep_ref, send_ref), rest = rest[:5], rest[5:10], rest[10:13], rest[13:]
    plan_ref, bounds_ref, table_ref, kv_ref, dkv_ref, dq_sum, dq_out, keep_out, lanes_ref, sums_ref, *buffers, sems = rest
    y, x, c = lax.axis_index("y"), lax.axis_index("x"), lax.axis_index("c")
    factor = HEAD_DIM ** (-0.5)

    small = [
        pltpu.make_async_copy(plan_in, plan_ref, sems.at[10]),
        pltpu.make_async_copy(bounds_in, bounds_ref, sems.at[11]),
    ]
    for copy in small:
        copy.start()
    copies = []
    for i, (slab, tile, count) in enumerate(PIECES):
        for core, sources in enumerate((mine, other)):
            rows = pl.ds(slab * 16 + core * 8 + tile, count)
            copies.append(pltpu.make_async_copy(sources[i], kv_ref.at[rows], sems.at[2 * i + core]))
    for copy in copies:
        copy.start()

    dkv_ref[...] = jnp.zeros_like(dkv_ref)
    dq_sum[...] = jnp.zeros_like(dq_sum)
    for buffer in buffers[2:]:
        buffer[...] = jnp.zeros_like(buffer)
    for copy in small:
        copy.wait()
    slabs = [((i - x) & 3) * 16 for i in range(4)]
    cores = [c * 8, (1 - c) * 8]
    for slot in range(64):
        place = slabs[slot // 4 % 4] + cores[slot // 2 % 2] + slot // 16 * 2 + slot % 2
        table_ref[plan_ref[slot // 2, slot % 2]] = place
    row = lax.broadcasted_iota(jnp.int32, (SPAN, LANES), 0)
    lane = lax.broadcasted_iota(jnp.int32, (1, LANES), 1)
    within = (lane // 256) * HALF + lane % HALF
    bounds = [bounds_ref[i] for i in range(1, 12)]
    steps = jnp.int32(0)
    for s in range(8):
        span = plan_ref[(s // 2) * 8 + x * 2 + c, s % 2]
        last = span * SPAN + within
        first = jnp.zeros_like(last)
        first_doc = jnp.int32(0)
        for bound in bounds:
            first = jnp.where(bound <= last, jnp.maximum(first, bound), first)
            first_doc = jnp.where(bound <= span * SPAN, jnp.maximum(first_doc, bound), first_doc)
        begin = lax.shift_right_logical(first_doc, 7)
        table_ref[QUERY + s] = span
        table_ref[BEGIN + s] = begin
        steps = steps + lax.shift_right_logical(span - begin + GROUP, 1)
        lanes_ref[s, 0:1] = first
        lanes_ref[s, 1:2] = last
        norms = packed_ref[s // 2 * 4 + y, 2 * HEAD_DIM : PACKED].astype(jnp.float32)
        rows = [slice(2 + s % 2 * 2 + i, 3 + s % 2 * 2 + i) for i in range(2)]
        norms = [norms[r] + norms[r.start + 4 : r.stop + 4] + norms[r.start + 8 : r.stop + 8] for r in rows]
        sums_ref[s, 0:1] = jnp.concatenate(norms, axis=1) * LOG2E
        parts = [packed_ref[2 * s + i, 2 * HEAD_DIM : PACKED].astype(jnp.float32) for i in range(2)]
        sums_ref[s, 1:2] = jnp.concatenate([part[0:1] + part[1:2] for part in parts], axis=1)
    for copy in copies:
        copy.wait()

    def operand(s, start):
        return jnp.concatenate([packed_ref[2 * s + i, start : start + HEAD_DIM] for i in range(2)], axis=1)

    def tiles_of(item):
        s, span = item
        return [table_ref[jnp.minimum(span + j, table_ref[QUERY + s])] for j in range(GROUP)]

    def tile(item, i):
        return jnp.concatenate([kv_ref[t, :, i].reshape(SPAN, HEAD_DIM) for t in tiles_of(item)], axis=0)

    def scores_stage(item, live, probs_ref, dscore_ref):
        s, span = item
        first, last = lanes_ref[s, 0:1], lanes_ref[s, 1:2]
        lse, delta = sums_ref[s, 0:1], sums_ref[s, 1:2]
        width = (last - first).astype(jnp.uint32)
        masks = []
        for j in range(GROUP):
            base = jnp.where(live & (span + j <= table_ref[QUERY + s]), (span + j) * SPAN, 8192)
            masks.append((row + (base - first)).astype(jnp.uint32) <= width)
        allowed = jnp.concatenate(masks, axis=0)
        scores = dot(tile(item, 0), operand(s, 0), 1, 0)
        probs = jnp.where(allowed, jnp.exp2(scores * (factor * LOG2E) - lse), 0.0)
        dprob = dot(tile(item, 1), operand(s, HEAD_DIM), 1, 0)
        probs_ref[...] = probs.astype(jnp.bfloat16)
        dscore_ref[...] = (probs * (dprob - delta)).astype(jnp.bfloat16)

    def sums_stage(item, probs_ref, dscore_ref):
        s, span = item
        probs, dscore = probs_ref[...], dscore_ref[...]
        part_v = dot(operand(s, HEAD_DIM), probs, 1, 1)
        part_k = dot(operand(s, 0), dscore, 1, 1)
        dq_sum[s] += dot(tile(item, 0), dscore, 0, 0)
        for i, part in ((0, part_k), (1, part_v)):
            for j, t in enumerate(tiles_of(item)):
                dkv_ref[t, i] += part[:, j * SPAN : (j + 1) * SPAN]

    def advance(item):
        s, span = item
        done = span + GROUP > table_ref[QUERY + s]
        following = jnp.where(done, jnp.minimum(s + 1, 7), s)
        return following, jnp.where(done, table_ref[BEGIN + following], span + GROUP)

    def two_steps(i, carry):
        before, item = carry
        scores_stage(item, True, buffers[0], buffers[1])
        sums_stage(before, buffers[2], buffers[3])
        following = advance(item)
        scores_stage(following, 2 * i + 1 < steps, buffers[2], buffers[3])
        sums_stage(item, buffers[0], buffers[1])
        return following, advance(following)

    start = (jnp.int32(0), table_ref[BEGIN])
    final, _ = lax.fori_loop(0, lax.shift_right_logical(steps + 1, 1), two_steps, (start, start))
    sums_stage(final, buffers[2], buffers[3])

    leaving = []

    def leave(source, target, sem):
        leaving.append(pltpu.make_async_copy(source, target, sem))
        leaving[-1].start()

    for i in range(16):
        lanes = slice((i % 2) * 256, (i % 2) * 256 + 256)
        dq_out[i] = (dq_sum[i // 2, :, lanes] * factor).astype(jnp.bfloat16)
    leave(dq_out, dq_ref, sems.at[12])
    for core in range(2):
        for slab in (2, 1, 3, 0):
            for t in range(8):
                start = slab * 16 + core * 8 + t
                key = (dkv_ref[start, 0] * factor).astype(jnp.bfloat16)
                value = dkv_ref[start, 1].astype(jnp.bfloat16)
                if core == 0:
                    keep_out[slab, t, 0], keep_out[slab, t, 1] = key, value
                else:
                    send_ref[slab, t, 0], send_ref[slab, t, 1] = key, value
            if core == 0:
                leave(keep_out.at[slab], keep_ref.at[slab], sems.at[13 + slab])
    for copy in leaving:
        copy.wait()


VMEM = pl.BlockSpec(memory_space=pltpu.VMEM)
HBM = pl.BlockSpec(memory_space=pltpu.HBM)


def tiles(plan, bounds, packed, mine, other):
    bf16, f32 = jnp.bfloat16, jnp.float32
    sums = (4, 8, 2, HEAD_DIM, SPAN)
    return pl.pallas_call(
        tiles_kernel,
        out_shape=[pltpu.HBM((16, HEAD_DIM, 256), bf16), pltpu.HBM(sums, bf16), jax.ShapeDtypeStruct(sums, bf16)],
        in_specs=[HBM] * 2 + [VMEM] + [pl.BlockSpec(memory_space=pl.ANY)] * 10,
        out_specs=[HBM, HBM, VMEM],
        scratch_shapes=[
            pltpu.SMEM((32, 2), jnp.int32),
            pltpu.SMEM((12,), jnp.int32),
            pltpu.SMEM((TABLE,), jnp.int32),
            pltpu.VMEM((64, 2, 2, HALF, HEAD_DIM), bf16),
            pltpu.VMEM((64, 2, HEAD_DIM, SPAN), f32),
            pltpu.VMEM((8, HEAD_DIM, LANES), f32),
            pltpu.VMEM((16, HEAD_DIM, 256), bf16),
            pltpu.VMEM((4, 8, 2, HEAD_DIM, SPAN), bf16),
            pltpu.VMEM((8, 2, LANES), jnp.int32),
            pltpu.VMEM((8, 2, LANES), f32),
        ]
        + [pltpu.VMEM((GROUP * SPAN, LANES), bf16)] * 4
        + [pltpu.SemaphoreType.DMA((17,))],
        compiler_params=pltpu.CompilerParams(vmem_limit_bytes=26 * MIB),
        name="tiles",
    )(plan, bounds, packed, *[part.reshape(-1, 2, 2, HALF, HEAD_DIM) for part in (*mine, *other)])


def shift(array, axis, by):
    return lax.ppermute(array, axis, [(i, (i + by) % 4) for i in range(4)])


def in_hbm(array):
    return pltpu.with_memory_space_constraint(array, pltpu.HBM)


def swap(array):
    return lax.ppermute(array, "c", [(0, 1), (1, 0)])


def exchange(array):
    return lax.all_to_all(array, ("z", "y"), 0, 0, tiled=True)


def shards(queries, keys, values, fwd_out, out_grad, log_norm, doc_bounds, span_plan, read_lists):
    bf16 = jnp.bfloat16
    f32 = jnp.float32

    kv_out = pl.pallas_call(
        pack_kv_kernel,
        out_shape=jax.ShapeDtypeStruct((4, 4, 2, HALF, HEAD_DIM), bf16),
        in_specs=[VMEM, VMEM],
        out_specs=VMEM,
        name="pack_kv",
    )(keys, values)
    block = exchange(kv_out.reshape(16, 2, HALF, HEAD_DIM))

    norms = log_norm.reshape(4, HALF, 4, 4).transpose(2, 0, 3, 1).reshape(4, 4, 256)
    wide = pl.BlockSpec((HALF, 16 * HEAD_DIM), lambda y: (0, y))
    q_out = pl.pallas_call(
        pack_q_kernel,
        grid=(4,),
        out_shape=jax.ShapeDtypeStruct((4, 4, PACKED, 256), bf16),
        in_specs=[wide, wide, wide, pl.BlockSpec((4, 4, 256), lambda y: (0, 0, 0))],
        out_specs=pl.BlockSpec((4, 1, PACKED, 256), lambda y: (0, y, 0, 0)),
        name="pack_q",
    )(queries, out_grad, fwd_out, norms)
    packed = exchange(q_out.reshape(16, PACKED, 256))

    from_next = shift(block, "x", -1)
    from_last = shift(block, "x", 1)
    far_a = shift(from_next[:8], "x", -1)
    far_b = shift(from_last[8:], "x", 1)

    plan, bounds = in_hbm(span_plan), in_hbm(doc_bounds)
    mine = [block, from_next, far_a, far_b, from_last]
    other = [swap(part) for part in mine]
    dq, keep, send = tiles(plan, bounds, packed, mine, other)

    got = swap(send)

    def block_of(slab, half):
        return pl.BlockSpec((1, 4, 2, HEAD_DIM, SPAN), lambda _: (slab, half, 0, 0, 0))

    piece = jax.ShapeDtypeStruct((1, 4, 2, HEAD_DIM, SPAN), bf16)
    via_next, via_last, last_b, next_a = pl.pallas_call(
        functools.partial(add_kernel, 2),
        grid=(1,),
        out_shape=[piece] * 4,
        in_specs=[block_of(*place) for place in ((2, 0), (2, 1), (1, 1), (3, 0)) for _ in range(2)],
        out_specs=[block_of(0, 0)] * 4,
        compiler_params=pltpu.CompilerParams(vmem_limit_bytes=8 * MIB),
        name="first_sums",
    )(*[keep, got] * 4)
    via_next, via_last = shift(via_next, "x", 1), shift(via_last, "x", -1)
    last_b, next_a = shift(last_b, "x", 1), shift(next_a, "x", -1)
    last_a, next_b = pl.pallas_call(
        functools.partial(add_kernel, 3),
        grid=(1,),
        out_shape=[piece] * 2,
        in_specs=[block_of(1, 0)] * 2 + [block_of(0, 0)] + [block_of(3, 1)] * 2 + [block_of(0, 0)],
        out_specs=[block_of(0, 0)] * 2,
        compiler_params=pltpu.CompilerParams(vmem_limit_bytes=6 * MIB),
        name="second_sums",
    )(keep, got, via_next, keep, got, via_last)
    last_a, next_b = shift(last_a, "x", 1), shift(next_b, "x", -1)
    dq_back = exchange(dq).reshape(4, 4, HEAD_DIM, 256)
    slab = pl.BlockSpec((1, 8, 2, HEAD_DIM, SPAN), lambda _: (0, 0, 0, 0, 0))
    total = pl.pallas_call(
        final_kernel,
        grid=(1,),
        out_shape=jax.ShapeDtypeStruct((16, 2, HALF, HEAD_DIM), bf16),
        in_specs=[slab] * 2 + [block_of(0, 0)] * 4,
        out_specs=pl.BlockSpec((16, 2, HALF, HEAD_DIM), lambda _: (0, 0, 0, 0)),
        compiler_params=pltpu.CompilerParams(vmem_limit_bytes=8 * MIB),
        name="own_slab",
    )(keep, got, last_a, last_b, next_a, next_b)
    total, dq_back = lax.optimization_barrier((total, dq_back))
    kv_back = exchange(total)
    grad_queries = pl.pallas_call(
        unpack_q_kernel,
        grid=(4,),
        out_shape=jax.ShapeDtypeStruct((HALF, 64 * HEAD_DIM), bf16),
        in_specs=[pl.BlockSpec((4, 1, HEAD_DIM, 256), lambda y: (0, y, 0, 0))],
        out_specs=wide,
        compiler_params=pltpu.CompilerParams(vmem_limit_bytes=6 * MIB),
        name="unpack_q",
    )(dq_back)
    grad_keys, grad_values = pl.pallas_call(
        unpack_kv_kernel,
        out_shape=[jax.ShapeDtypeStruct((HALF, 8 * HEAD_DIM), bf16)] * 2,
        in_specs=[VMEM],
        out_specs=[VMEM, VMEM],
        compiler_params=pltpu.CompilerParams(vmem_limit_bytes=4 * MIB),
        name="unpack_kv",
    )(kv_back.reshape(4, 4, 2, HALF, HEAD_DIM))
    return (grad_queries, grad_keys, grad_values)


def solution(mesh):
    fine = Mesh(mesh.devices.reshape(4, 4, 2, 4), ROWS)
    rows = P(ROWS, None)
    cp = ("z", "x", "c")
    in_specs = (rows, rows, rows, rows, rows, P(cp, "y"), P(), P(), P(cp, None, None))
    return jax.shard_map(shards, mesh=fine, in_specs=in_specs, out_specs=(rows, rows, rows), check_vma=False)
```

```python
import functools

import jax
import jax.numpy as jnp
from jax import lax
from jax.experimental import pallas as pl
from jax.experimental.pallas import tpu as pltpu
from jax.sharding import Mesh, PartitionSpec as P

HEAD_DIM = 128
SPAN = 128
HALF = 64
LOG2E = 1.4426950408889634
LANES = 512
PACKED = 272
ROWS = ("z", "x", "c", "y")
MIB = 1024 * 1024


def dot(a, b, ca, cb):
    return lax.dot_general(a, b, (((ca,), (cb,)), ((), ())), preferred_element_type=jnp.float32)


def pack_kv_kernel(keys_ref, values_ref, out_ref):
    for z in range(4):
        for y in range(4):
            cols = slice((2 * y + z // 2) * HEAD_DIM, (2 * y + z // 2 + 1) * HEAD_DIM)
            out_ref[y, z, 0] = keys_ref[:, cols]
            out_ref[y, z, 1] = values_ref[:, cols]


def pack_q_kernel(queries_ref, grad_ref, fwd_ref, norms_ref, out_ref):
    row = lax.broadcasted_iota(jnp.int32, (16, HEAD_DIM), 0)
    pick = (row < 2).astype(jnp.bfloat16)
    for z in range(4):
        for pair in range(2):
            cols = [slice((z * 4 + 2 * pair + i) * HEAD_DIM, (z * 4 + 2 * pair + i + 1) * HEAD_DIM) for i in range(2)]
            lanes = slice(pair * HEAD_DIM, (pair + 1) * HEAD_DIM)
            query = jnp.concatenate([queries_ref[:, col] for col in cols], axis=0)
            grad = jnp.concatenate([grad_ref[:, col] for col in cols], axis=0)
            fwd = jnp.concatenate([fwd_ref[:, col] for col in cols], axis=0)
            out_ref[0, z, 0:HEAD_DIM, lanes] = jnp.transpose(query)
            out_ref[0, z, HEAD_DIM : 2 * HEAD_DIM, lanes] = jnp.transpose(grad)
            product = grad.astype(jnp.float32) * fwd.astype(jnp.float32)
            high = product.astype(jnp.bfloat16)
            low = (product - high.astype(jnp.float32)).astype(jnp.bfloat16)
            delta = dot(pick, high, 1, 1) + dot(pick, low, 1, 1)
            high = delta.astype(jnp.bfloat16).astype(jnp.float32)
            pieces, rest = [], norms_ref[z, :, lanes]
            for _ in range(3):
                pieces.append(rest.astype(jnp.bfloat16).astype(jnp.float32))
                rest = rest - pieces[-1]
            tail = jnp.concatenate([high[0:1], (delta - high)[1:2], *pieces, high[0:2]], axis=0)
            out_ref[0, z, 2 * HEAD_DIM : PACKED, lanes] = tail.astype(jnp.bfloat16)


def unpack_q_kernel(in_ref, out_ref):
    for z in range(4):
        for pair in range(2):
            part = jnp.transpose(in_ref[0, z, :, pair * HEAD_DIM : (pair + 1) * HEAD_DIM])
            for i in range(2):
                head = z * 4 + 2 * pair + i
                out_ref[:, head * HEAD_DIM : (head + 1) * HEAD_DIM] = part[i * HALF : (i + 1) * HALF]


def add_kernel(terms, *refs):
    count = len(refs) // (terms + 1)
    for i in range(count):
        for t in range(4):
            total = refs[i * terms][0, t].astype(jnp.float32)
            for k in range(1, terms):
                total = total + refs[i * terms + k][0, t].astype(jnp.float32)
            refs[count * terms + i][0, t] = total.astype(jnp.bfloat16)


def final_kernel(keep_ref, got_ref, last_a_ref, last_b_ref, next_a_ref, next_b_ref, out_ref):
    for t in range(8):
        last_ref, next_ref = ((last_a_ref, next_a_ref), (last_b_ref, next_b_ref))[t // 4]
        for i in range(2):
            total = keep_ref[0, t, i].astype(jnp.float32) + got_ref[0, t, i].astype(jnp.float32)
            total = total + last_ref[0, t % 4, i].astype(jnp.float32) + next_ref[0, t % 4, i].astype(jnp.float32)
            rows = jnp.transpose(total).astype(jnp.bfloat16)
            first = t // 4 * 8 + t % 4
            out_ref[first, i] = rows[:HALF]
            out_ref[first + 4, i] = rows[HALF:]


def unpack_kv_kernel(in_ref, keys_ref, values_ref):
    for g in range(8):
        cols = slice(g * HEAD_DIM, (g + 1) * HEAD_DIM)
        y, z = g // 2, 2 * (g % 2)
        for i, out_ref in ((0, keys_ref), (1, values_ref)):
            total = in_ref[y, z, i].astype(jnp.float32) + in_ref[y, z + 1, i].astype(jnp.float32)
            out_ref[:, cols] = total.astype(jnp.bfloat16)


PIECES = ((0, 0, 8), (1, 0, 8), (2, 0, 4), (2, 4, 4), (3, 0, 8))
GROUP = 2
QUERY, BEGIN, TABLE = 64, 72, 80


def tiles_kernel(plan_in, bounds_in, packed_ref, *rest):
    mine, other, (dq_ref, keep_ref, send_ref), rest = rest[:5], rest[5:10], rest[10:13], rest[13:]
    plan_ref, bounds_ref, table_ref, kv_ref, dkv_ref, dq_sum, dq_out, keep_out, lanes_ref, sums_ref, *buffers, sems = rest
    y, x, c = lax.axis_index("y"), lax.axis_index("x"), lax.axis_index("c")
    factor = HEAD_DIM ** (-0.5)

    small = [
        pltpu.make_async_copy(plan_in, plan_ref, sems.at[10]),
        pltpu.make_async_copy(bounds_in, bounds_ref, sems.at[11]),
    ]
    for copy in small:
        copy.start()
    copies = []
    for i, (slab, tile, count) in enumerate(PIECES):
        for core, sources in enumerate((mine, other)):
            rows = pl.ds((slab * 16 + core * 8 + tile) // 4, count // 4)
            copies.append(pltpu.make_async_copy(sources[i], kv_ref.at[rows], sems.at[2 * i + core]))
    for copy in copies:
        copy.start()

    dkv_ref[...] = jnp.zeros_like(dkv_ref)
    dq_sum[...] = jnp.zeros_like(dq_sum)
    for buffer in buffers[2:]:
        buffer[...] = jnp.zeros_like(buffer)
    for copy in small:
        copy.wait()
    slabs = [((i - x) & 3) * 16 for i in range(4)]
    cores = [c * 8, (1 - c) * 8]
    for slot in range(64):
        place = slabs[slot // 4 % 4] + cores[slot // 2 % 2] + slot % 2 * 4 + slot // 16
        table_ref[plan_ref[slot // 2, slot % 2]] = place
    row = lax.broadcasted_iota(jnp.int32, (SPAN, LANES), 0)
    lane = lax.broadcasted_iota(jnp.int32, (1, LANES), 1)
    within = (lane // 256) * HALF + lane % HALF
    bounds = [bounds_ref[i] for i in range(1, 12)]
    steps = jnp.int32(0)
    for s in range(8):
        span = plan_ref[(s // 2) * 8 + x * 2 + c, s % 2]
        last = span * SPAN + within
        first = jnp.zeros_like(last)
        first_doc = jnp.int32(0)
        for bound in bounds:
            first = jnp.where(bound <= last, jnp.maximum(first, bound), first)
            first_doc = jnp.where(bound <= span * SPAN, jnp.maximum(first_doc, bound), first_doc)
        begin = lax.shift_right_logical(first_doc, 7)
        table_ref[QUERY + s] = span
        table_ref[BEGIN + s] = begin
        steps = steps + lax.shift_right_logical(span - begin + GROUP, 1)
        lanes_ref[s, 0:1] = first
        lanes_ref[s, 1:2] = last
        norms = packed_ref[y * 4 + s // 2, 2 * HEAD_DIM : PACKED].astype(jnp.float32)
        rows = [slice(2 + s % 2 * 2 + i, 3 + s % 2 * 2 + i) for i in range(2)]
        norms = [norms[r] + norms[r.start + 4 : r.stop + 4] + norms[r.start + 8 : r.stop + 8] for r in rows]
        sums_ref[s, 0:1] = jnp.concatenate(norms, axis=1) * LOG2E
        parts = [packed_ref[(s % 2 * 2 + i) * 4 + s // 2, 2 * HEAD_DIM : PACKED].astype(jnp.float32) for i in range(2)]
        sums_ref[s, 1:2] = jnp.concatenate([part[0:1] + part[1:2] for part in parts], axis=1)
    for copy in copies:
        copy.wait()

    def operand(s, start):
        first = (s & 1) * 8 + lax.shift_right_logical(s, 1)
        return jnp.concatenate([packed_ref[first + 4 * i, start : start + HEAD_DIM] for i in range(2)], axis=1)

    def tiles_of(item):
        s, span = item
        return [table_ref[jnp.minimum(span + j, table_ref[QUERY + s])] for j in range(GROUP)]

    def tile(item, i):
        return jnp.concatenate([kv_ref[lax.shift_right_logical(t, 2), :, t & 3, i].reshape(SPAN, HEAD_DIM) for t in tiles_of(item)], axis=0)

    def scores_stage(item, live, probs_ref, dscore_ref):
        s, span = item
        first, last = lanes_ref[s, 0:1], lanes_ref[s, 1:2]
        lse, delta = sums_ref[s, 0:1], sums_ref[s, 1:2]
        width = (last - first).astype(jnp.uint32)
        masks = []
        for j in range(GROUP):
            base = jnp.where(live & (span + j <= table_ref[QUERY + s]), (span + j) * SPAN, 8192)
            masks.append((row + (base - first)).astype(jnp.uint32) <= width)
        allowed = jnp.concatenate(masks, axis=0)
        scores = dot(tile(item, 0), operand(s, 0), 1, 0)
        probs = jnp.where(allowed, jnp.exp2(scores * (factor * LOG2E) - lse), 0.0)
        dprob = dot(tile(item, 1), operand(s, HEAD_DIM), 1, 0)
        probs_ref[...] = probs.astype(jnp.bfloat16)
        dscore_ref[...] = (probs * (dprob - delta)).astype(jnp.bfloat16)

    def sums_stage(item, probs_ref, dscore_ref):
        s, span = item
        probs, dscore = probs_ref[...], dscore_ref[...]
        part_v = dot(operand(s, HEAD_DIM), probs, 1, 1)
        part_k = dot(operand(s, 0), dscore, 1, 1)
        dq_sum[s] += dot(tile(item, 0), dscore, 0, 0)
        for i, part in ((0, part_k), (1, part_v)):
            for j, t in enumerate(tiles_of(item)):
                dkv_ref[t, i] += part[:, j * SPAN : (j + 1) * SPAN]

    def advance(item):
        s, span = item
        done = span + GROUP > table_ref[QUERY + s]
        following = jnp.where(done, jnp.minimum(s + 1, 7), s)
        return following, jnp.where(done, table_ref[BEGIN + following], span + GROUP)

    def two_steps(i, carry):
        before, item = carry
        scores_stage(item, True, buffers[0], buffers[1])
        sums_stage(before, buffers[2], buffers[3])
        following = advance(item)
        scores_stage(following, 2 * i + 1 < steps, buffers[2], buffers[3])
        sums_stage(item, buffers[0], buffers[1])
        return following, advance(following)

    start = (jnp.int32(0), table_ref[BEGIN])
    final, _ = lax.fori_loop(0, lax.shift_right_logical(steps + 1, 1), two_steps, (start, start))
    sums_stage(final, buffers[2], buffers[3])

    leaving = []

    def leave(source, target, sem):
        leaving.append(pltpu.make_async_copy(source, target, sem))
        leaving[-1].start()

    for i in range(16):
        lanes = slice((i % 2) * 256, (i % 2) * 256 + 256)
        dq_out[(i // 2 % 2 * 2 + i % 2) * 4 + i // 4] = (dq_sum[i // 2, :, lanes] * factor).astype(jnp.bfloat16)
    leave(dq_out, dq_ref, sems.at[12])
    for core in range(2):
        for slab in (2, 1, 3, 0):
            for t in range(8):
                start = slab * 16 + core * 8 + t
                key = (dkv_ref[start, 0] * factor).astype(jnp.bfloat16)
                value = dkv_ref[start, 1].astype(jnp.bfloat16)
                if core == 0:
                    keep_out[slab, t, 0], keep_out[slab, t, 1] = key, value
                else:
                    send_ref[slab, t, 0], send_ref[slab, t, 1] = key, value
            if core == 0:
                leave(keep_out.at[slab], keep_ref.at[slab], sems.at[13 + slab])
    for copy in leaving:
        copy.wait()


VMEM = pl.BlockSpec(memory_space=pltpu.VMEM)
HBM = pl.BlockSpec(memory_space=pltpu.HBM)


def tiles(plan, bounds, packed, mine, other):
    bf16, f32 = jnp.bfloat16, jnp.float32
    sums = (4, 8, 2, HEAD_DIM, SPAN)
    return pl.pallas_call(
        tiles_kernel,
        out_shape=[pltpu.HBM((16, HEAD_DIM, 256), bf16), pltpu.HBM(sums, bf16), jax.ShapeDtypeStruct(sums, bf16)],
        in_specs=[HBM] * 2 + [VMEM] + [pl.BlockSpec(memory_space=pl.ANY)] * 10,
        out_specs=[HBM, HBM, VMEM],
        scratch_shapes=[
            pltpu.SMEM((32, 2), jnp.int32),
            pltpu.SMEM((12,), jnp.int32),
            pltpu.SMEM((TABLE,), jnp.int32),
            pltpu.VMEM((16, 2, 4, 2, HALF, HEAD_DIM), bf16),
            pltpu.VMEM((64, 2, HEAD_DIM, SPAN), f32),
            pltpu.VMEM((8, HEAD_DIM, LANES), f32),
            pltpu.VMEM((16, HEAD_DIM, 256), bf16),
            pltpu.VMEM((4, 8, 2, HEAD_DIM, SPAN), bf16),
            pltpu.VMEM((8, 2, LANES), jnp.int32),
            pltpu.VMEM((8, 2, LANES), f32),
        ]
        + [pltpu.VMEM((GROUP * SPAN, LANES), bf16)] * 4
        + [pltpu.SemaphoreType.DMA((17,))],
        compiler_params=pltpu.CompilerParams(vmem_limit_bytes=26 * MIB),
        name="tiles",
    )(plan, bounds, packed, *[part.reshape(-1, 2, 4, 2, HALF, HEAD_DIM) for part in (*mine, *other)])


def shift(array, axis, by):
    return lax.ppermute(array, axis, [(i, (i + by) % 4) for i in range(4)])


def in_hbm(array):
    return pltpu.with_memory_space_constraint(array, pltpu.HBM)


def swap(array):
    return lax.ppermute(array, "c", [(0, 1), (1, 0)])


def exchange(array):
    return lax.all_to_all(array, ("y", "z"), 0, 0, tiled=True)


def shards(queries, keys, values, fwd_out, out_grad, log_norm, doc_bounds, span_plan, read_lists):
    bf16 = jnp.bfloat16
    f32 = jnp.float32

    kv_out = pl.pallas_call(
        pack_kv_kernel,
        out_shape=jax.ShapeDtypeStruct((4, 4, 2, HALF, HEAD_DIM), bf16),
        in_specs=[VMEM, VMEM],
        out_specs=VMEM,
        name="pack_kv",
    )(keys, values)
    block = exchange(kv_out.reshape(16, 2, HALF, HEAD_DIM))

    norms = log_norm.reshape(4, HALF, 4, 4).transpose(2, 0, 3, 1).reshape(4, 4, 256)
    wide = pl.BlockSpec((HALF, 16 * HEAD_DIM), lambda y: (0, y))
    q_out = pl.pallas_call(
        pack_q_kernel,
        grid=(4,),
        out_shape=jax.ShapeDtypeStruct((4, 4, PACKED, 256), bf16),
        in_specs=[wide, wide, wide, pl.BlockSpec((4, 4, 256), lambda y: (0, 0, 0))],
        out_specs=pl.BlockSpec((1, 4, PACKED, 256), lambda y: (y, 0, 0, 0)),
        name="pack_q",
    )(queries, out_grad, fwd_out, norms)
    packed = exchange(q_out.reshape(16, PACKED, 256))

    from_next = shift(block, "x", -1)
    from_last = shift(block, "x", 1)
    far_a = shift(from_next[:8], "x", -1)
    far_b = shift(from_last[8:], "x", 1)

    plan, bounds = in_hbm(span_plan), in_hbm(doc_bounds)
    mine = [block, from_next, far_a, far_b, from_last]
    other = [swap(part) for part in mine]
    dq, keep, send = tiles(plan, bounds, packed, mine, other)

    got = swap(send)

    def block_of(slab, half):
        return pl.BlockSpec((1, 4, 2, HEAD_DIM, SPAN), lambda _: (slab, half, 0, 0, 0))

    piece = jax.ShapeDtypeStruct((1, 4, 2, HEAD_DIM, SPAN), bf16)
    via_next, via_last, last_b, next_a = pl.pallas_call(
        functools.partial(add_kernel, 2),
        grid=(1,),
        out_shape=[piece] * 4,
        in_specs=[block_of(*place) for place in ((2, 0), (2, 1), (1, 1), (3, 0)) for _ in range(2)],
        out_specs=[block_of(0, 0)] * 4,
        compiler_params=pltpu.CompilerParams(vmem_limit_bytes=8 * MIB),
        name="first_sums",
    )(*[keep, got] * 4)
    via_next, via_last = shift(via_next, "x", 1), shift(via_last, "x", -1)
    last_b, next_a = shift(last_b, "x", 1), shift(next_a, "x", -1)
    last_a, next_b = pl.pallas_call(
        functools.partial(add_kernel, 3),
        grid=(1,),
        out_shape=[piece] * 2,
        in_specs=[block_of(1, 0)] * 2 + [block_of(0, 0)] + [block_of(3, 1)] * 2 + [block_of(0, 0)],
        out_specs=[block_of(0, 0)] * 2,
        compiler_params=pltpu.CompilerParams(vmem_limit_bytes=6 * MIB),
        name="second_sums",
    )(keep, got, via_next, keep, got, via_last)
    last_a, next_b = shift(last_a, "x", 1), shift(next_b, "x", -1)
    dq_back = exchange(dq).reshape(4, 4, HEAD_DIM, 256)
    slab = pl.BlockSpec((1, 8, 2, HEAD_DIM, SPAN), lambda _: (0, 0, 0, 0, 0))
    total = pl.pallas_call(
        final_kernel,
        grid=(1,),
        out_shape=jax.ShapeDtypeStruct((16, 2, HALF, HEAD_DIM), bf16),
        in_specs=[slab] * 2 + [block_of(0, 0)] * 4,
        out_specs=pl.BlockSpec((16, 2, HALF, HEAD_DIM), lambda _: (0, 0, 0, 0)),
        compiler_params=pltpu.CompilerParams(vmem_limit_bytes=8 * MIB),
        name="own_slab",
    )(keep, got, last_a, last_b, next_a, next_b)
    total, dq_back = lax.optimization_barrier((total, dq_back))
    kv_back = exchange(total)
    grad_queries = pl.pallas_call(
        unpack_q_kernel,
        grid=(4,),
        out_shape=jax.ShapeDtypeStruct((HALF, 64 * HEAD_DIM), bf16),
        in_specs=[pl.BlockSpec((1, 4, HEAD_DIM, 256), lambda y: (y, 0, 0, 0))],
        out_specs=wide,
        compiler_params=pltpu.CompilerParams(vmem_limit_bytes=6 * MIB),
        name="unpack_q",
    )(dq_back)
    grad_keys, grad_values = pl.pallas_call(
        unpack_kv_kernel,
        out_shape=[jax.ShapeDtypeStruct((HALF, 8 * HEAD_DIM), bf16)] * 2,
        in_specs=[VMEM],
        out_specs=[VMEM, VMEM],
        compiler_params=pltpu.CompilerParams(vmem_limit_bytes=4 * MIB),
        name="unpack_kv",
    )(kv_back.reshape(4, 4, 2, HALF, HEAD_DIM))
    return (grad_queries, grad_keys, grad_values)


def solution(mesh):
    fine = Mesh(mesh.devices.reshape(4, 4, 2, 4), ROWS)
    rows = P(ROWS, None)
    cp = ("z", "x", "c")
    in_specs = (rows, rows, rows, rows, rows, P(cp, "y"), P(), P(), P(cp, None, None))
    return jax.shard_map(shards, mesh=fine, in_specs=in_specs, out_specs=(rows, rows, rows), check_vma=False)
```

```python
import functools

import jax
import jax.numpy as jnp
from jax import lax
from jax.experimental import pallas as pl
from jax.experimental.pallas import tpu as pltpu
from jax.sharding import Mesh, PartitionSpec as P

HEAD_DIM = 128
SPAN = 128
HALF = 64
LOG2E = 1.4426950408889634
LANES = 512
PACKED = 272
ROWS = ("z", "x", "c", "y")
MIB = 1024 * 1024


def dot(a, b, ca, cb):
    return lax.dot_general(a, b, (((ca,), (cb,)), ((), ())), preferred_element_type=jnp.float32)


def pack_kv_kernel(keys_ref, values_ref, out_ref):
    for z in range(4):
        for y in range(2):
            cols = slice((2 * y + z // 2) * HEAD_DIM, (2 * y + z // 2 + 1) * HEAD_DIM)
            out_ref[y, z, 0] = keys_ref[:, cols]
            out_ref[y, z, 1] = values_ref[:, cols]


def pack_q_kernel(queries_ref, grad_ref, fwd_ref, norms_ref, out_ref):
    row = lax.broadcasted_iota(jnp.int32, (16, HEAD_DIM), 0)
    pick = (row < 2).astype(jnp.bfloat16)
    for z in range(4):
        for pair in range(2):
            cols = [slice((z * 4 + 2 * pair + i) * HEAD_DIM, (z * 4 + 2 * pair + i + 1) * HEAD_DIM) for i in range(2)]
            lanes = slice(pair * HEAD_DIM, (pair + 1) * HEAD_DIM)
            query = jnp.concatenate([queries_ref[:, col] for col in cols], axis=0)
            grad = jnp.concatenate([grad_ref[:, col] for col in cols], axis=0)
            fwd = jnp.concatenate([fwd_ref[:, col] for col in cols], axis=0)
            out_ref[0, z, 0:HEAD_DIM, lanes] = jnp.transpose(query)
            out_ref[0, z, HEAD_DIM : 2 * HEAD_DIM, lanes] = jnp.transpose(grad)
            product = grad.astype(jnp.float32) * fwd.astype(jnp.float32)
            high = product.astype(jnp.bfloat16)
            low = (product - high.astype(jnp.float32)).astype(jnp.bfloat16)
            delta = dot(pick, high, 1, 1) + dot(pick, low, 1, 1)
            high = delta.astype(jnp.bfloat16).astype(jnp.float32)
            pieces, rest = [], norms_ref[z, :, lanes]
            for _ in range(3):
                pieces.append(rest.astype(jnp.bfloat16).astype(jnp.float32))
                rest = rest - pieces[-1]
            tail = jnp.concatenate([high[0:1], (delta - high)[1:2], *pieces, high[0:2]], axis=0)
            out_ref[0, z, 2 * HEAD_DIM : PACKED, lanes] = tail.astype(jnp.bfloat16)


def unpack_q_kernel(in_ref, out_ref):
    for z in range(4):
        for pair in range(2):
            part = jnp.transpose(in_ref[0, z, :, pair * HEAD_DIM : (pair + 1) * HEAD_DIM])
            for i in range(2):
                head = z * 4 + 2 * pair + i
                out_ref[:, head * HEAD_DIM : (head + 1) * HEAD_DIM] = part[i * HALF : (i + 1) * HALF]


def add_kernel(terms, *refs):
    count = len(refs) // (terms + 1)
    for i in range(count):
        for t in range(4):
            total = refs[i * terms][0, t].astype(jnp.float32)
            for k in range(1, terms):
                total = total + refs[i * terms + k][0, t].astype(jnp.float32)
            refs[count * terms + i][0, t] = total.astype(jnp.bfloat16)


def final_kernel(keep_ref, got_ref, last_a_ref, last_b_ref, next_a_ref, next_b_ref, out_ref):
    def half(last_ref, next_ref):
        for t in range(4):
            for i in range(2):
                total = keep_ref[0, t, i].astype(jnp.float32) + got_ref[0, t, i].astype(jnp.float32)
                total = total + last_ref[0, t, i].astype(jnp.float32) + next_ref[0, t, i].astype(jnp.float32)
                rows = jnp.transpose(total).astype(jnp.bfloat16)
                out_ref[t, i] = rows[:HALF]
                out_ref[t + 4, i] = rows[HALF:]

    @pl.when(pl.program_id(0) == 0)
    def _():
        half(last_a_ref, next_a_ref)

    @pl.when(pl.program_id(0) == 1)
    def _():
        half(last_b_ref, next_b_ref)


def unpack_kv_kernel(in_ref, keys_ref, values_ref):
    for g in range(8):
        cols = slice(g * HEAD_DIM, (g + 1) * HEAD_DIM)
        y, z = g // 2, 2 * (g % 2)
        for i, out_ref in ((0, keys_ref), (1, values_ref)):
            total = in_ref[y, z, i].astype(jnp.float32) + in_ref[y, z + 1, i].astype(jnp.float32)
            out_ref[:, cols] = total.astype(jnp.bfloat16)


PIECES = ((0, 0, 8), (1, 0, 8), (2, 0, 4), (2, 4, 4), (3, 0, 8))
GROUP = 2
QUERY, BEGIN, TABLE = 64, 72, 80


def tiles_kernel(plan_in, bounds_in, packed_ref, *rest):
    mine, other, (dq_ref, keep_ref, send_ref), rest = rest[:5], rest[5:10], rest[10:13], rest[13:]
    plan_ref, bounds_ref, table_ref, kv_ref, dkv_ref, dq_sum, dq_out, keep_out, lanes_ref, sums_ref, *buffers, sems = rest
    y, x, c = lax.axis_index("y"), lax.axis_index("x"), lax.axis_index("c")
    factor = HEAD_DIM ** (-0.5)

    small = [
        pltpu.make_async_copy(plan_in, plan_ref, sems.at[10]),
        pltpu.make_async_copy(bounds_in, bounds_ref, sems.at[11]),
    ]
    for copy in small:
        copy.start()
    copies = []
    for i, (slab, tile, count) in enumerate(PIECES):
        for core, sources in enumerate((mine, other)):
            rows = pl.ds((slab * 16 + core * 8 + tile) // 4, count // 4)
            copies.append(pltpu.make_async_copy(sources[i], kv_ref.at[rows], sems.at[2 * i + core]))
    for copy in copies:
        copy.start()

    dkv_ref[...] = jnp.zeros_like(dkv_ref)
    dq_sum[...] = jnp.zeros_like(dq_sum)
    for buffer in buffers[2:]:
        buffer[...] = jnp.zeros_like(buffer)
    for copy in small:
        copy.wait()
    slabs = [((i - x) & 3) * 16 for i in range(4)]
    cores = [c * 8, (1 - c) * 8]
    for slot in range(64):
        place = slabs[slot // 4 % 4] + cores[slot // 2 % 2] + slot % 2 * 4 + slot // 16
        table_ref[plan_ref[slot // 2, slot % 2]] = place
    row = lax.broadcasted_iota(jnp.int32, (SPAN, LANES), 0)
    lane = lax.broadcasted_iota(jnp.int32, (1, LANES), 1)
    within = (lane // 256) * HALF + lane % HALF
    bounds = [bounds_ref[i] for i in range(1, 12)]
    steps = jnp.int32(0)
    for s in range(8):
        span = plan_ref[(s // 2) * 8 + x * 2 + c, s % 2]
        last = span * SPAN + within
        first = jnp.zeros_like(last)
        first_doc = jnp.int32(0)
        for bound in bounds:
            first = jnp.where(bound <= last, jnp.maximum(first, bound), first)
            first_doc = jnp.where(bound <= span * SPAN, jnp.maximum(first_doc, bound), first_doc)
        begin = lax.shift_right_logical(first_doc, 7)
        table_ref[QUERY + s] = span
        table_ref[BEGIN + s] = begin
        steps = steps + lax.shift_right_logical(span - begin + GROUP, 1)
        lanes_ref[s, 0:1] = first
        lanes_ref[s, 1:2] = last
        norms = packed_ref[y * 4 + s // 2, 2 * HEAD_DIM : PACKED].astype(jnp.float32)
        rows = [slice(2 + s % 2 * 2 + i, 3 + s % 2 * 2 + i) for i in range(2)]
        norms = [norms[r] + norms[r.start + 4 : r.stop + 4] + norms[r.start + 8 : r.stop + 8] for r in rows]
        sums_ref[s, 0:1] = jnp.concatenate(norms, axis=1) * LOG2E
        parts = [packed_ref[(s % 2 * 2 + i) * 4 + s // 2, 2 * HEAD_DIM : PACKED].astype(jnp.float32) for i in range(2)]
        sums_ref[s, 1:2] = jnp.concatenate([part[0:1] + part[1:2] for part in parts], axis=1)
    for copy in copies:
        copy.wait()

    def operand(s, start):
        first = (s & 1) * 8 + lax.shift_right_logical(s, 1)
        return jnp.concatenate([packed_ref[first + 4 * i, start : start + HEAD_DIM] for i in range(2)], axis=1)

    def tiles_of(item):
        s, span = item
        return [table_ref[jnp.minimum(span + j, table_ref[QUERY + s])] for j in range(GROUP)]

    def tile(item, i):
        return jnp.concatenate([kv_ref[lax.shift_right_logical(t, 2), :, t & 3, i].reshape(SPAN, HEAD_DIM) for t in tiles_of(item)], axis=0)

    def scores_stage(item, live, probs_ref, dscore_ref):
        s, span = item
        first, last = lanes_ref[s, 0:1], lanes_ref[s, 1:2]
        lse, delta = sums_ref[s, 0:1], sums_ref[s, 1:2]
        width = (last - first).astype(jnp.uint32)
        masks = []
        for j in range(GROUP):
            base = jnp.where(live & (span + j <= table_ref[QUERY + s]), (span + j) * SPAN, 8192)
            masks.append((row + (base - first)).astype(jnp.uint32) <= width)
        allowed = jnp.concatenate(masks, axis=0)
        scores = dot(tile(item, 0), operand(s, 0), 1, 0)
        probs = jnp.where(allowed, jnp.exp2(scores * (factor * LOG2E) - lse), 0.0)
        dprob = dot(tile(item, 1), operand(s, HEAD_DIM), 1, 0)
        probs_ref[...] = probs.astype(jnp.bfloat16)
        dscore_ref[...] = (probs * (dprob - delta)).astype(jnp.bfloat16)

    def sums_stage(item, probs_ref, dscore_ref):
        s, span = item
        probs, dscore = probs_ref[...], dscore_ref[...]
        part_v = dot(operand(s, HEAD_DIM), probs, 1, 1)
        part_k = dot(operand(s, 0), dscore, 1, 1)
        dq_sum[s] += dot(tile(item, 0), dscore, 0, 0)
        for i, part in ((0, part_k), (1, part_v)):
            for j, t in enumerate(tiles_of(item)):
                dkv_ref[t, i] += part[:, j * SPAN : (j + 1) * SPAN]

    def advance(item):
        s, span = item
        done = span + GROUP > table_ref[QUERY + s]
        following = jnp.where(done, jnp.minimum(s + 1, 7), s)
        return following, jnp.where(done, table_ref[BEGIN + following], span + GROUP)

    def two_steps(i, carry):
        before, item = carry
        scores_stage(item, True, buffers[0], buffers[1])
        sums_stage(before, buffers[2], buffers[3])
        following = advance(item)
        scores_stage(following, 2 * i + 1 < steps, buffers[2], buffers[3])
        sums_stage(item, buffers[0], buffers[1])
        return following, advance(following)

    start = (jnp.int32(0), table_ref[BEGIN])
    final, _ = lax.fori_loop(0, lax.shift_right_logical(steps + 1, 1), two_steps, (start, start))
    sums_stage(final, buffers[2], buffers[3])

    leaving = []

    def leave(source, target, sem):
        leaving.append(pltpu.make_async_copy(source, target, sem))
        leaving[-1].start()

    for i in range(16):
        lanes = slice((i % 2) * 256, (i % 2) * 256 + 256)
        dq_out[(i // 2 % 2 * 2 + i % 2) * 4 + i // 4] = (dq_sum[i // 2, :, lanes] * factor).astype(jnp.bfloat16)
    leave(dq_out, dq_ref, sems.at[12])
    for core in range(2):
        for slab in (2, 1, 3, 0):
            for t in range(8):
                start = slab * 16 + core * 8 + t
                key = (dkv_ref[start, 0] * factor).astype(jnp.bfloat16)
                value = dkv_ref[start, 1].astype(jnp.bfloat16)
                if core == 0:
                    keep_out[slab, t, 0], keep_out[slab, t, 1] = key, value
                else:
                    send_ref[slab, t, 0], send_ref[slab, t, 1] = key, value
            if core == 0:
                leave(keep_out.at[slab], keep_ref.at[slab], sems.at[13 + slab])
    for copy in leaving:
        copy.wait()


VMEM = pl.BlockSpec(memory_space=pltpu.VMEM)
HBM = pl.BlockSpec(memory_space=pltpu.HBM)


def tiles(plan, bounds, packed, mine, other):
    bf16, f32 = jnp.bfloat16, jnp.float32
    sums = (4, 8, 2, HEAD_DIM, SPAN)
    return pl.pallas_call(
        tiles_kernel,
        out_shape=[pltpu.HBM((16, HEAD_DIM, 256), bf16), pltpu.HBM(sums, bf16), jax.ShapeDtypeStruct(sums, bf16)],
        in_specs=[HBM] * 2 + [VMEM] + [pl.BlockSpec(memory_space=pl.ANY)] * 10,
        out_specs=[HBM, HBM, VMEM],
        scratch_shapes=[
            pltpu.SMEM((32, 2), jnp.int32),
            pltpu.SMEM((12,), jnp.int32),
            pltpu.SMEM((TABLE,), jnp.int32),
            pltpu.VMEM((16, 2, 4, 2, HALF, HEAD_DIM), bf16),
            pltpu.VMEM((64, 2, HEAD_DIM, SPAN), f32),
            pltpu.VMEM((8, HEAD_DIM, LANES), f32),
            pltpu.VMEM((16, HEAD_DIM, 256), bf16),
            pltpu.VMEM((4, 8, 2, HEAD_DIM, SPAN), bf16),
            pltpu.VMEM((8, 2, LANES), jnp.int32),
            pltpu.VMEM((8, 2, LANES), f32),
        ]
        + [pltpu.VMEM((GROUP * SPAN, LANES), bf16)] * 4
        + [pltpu.SemaphoreType.DMA((17,))],
        compiler_params=pltpu.CompilerParams(vmem_limit_bytes=26 * MIB),
        name="tiles",
    )(plan, bounds, packed, *[part.reshape(-1, 2, 4, 2, HALF, HEAD_DIM) for part in (*mine, *other)])


def shift(array, axis, by):
    return lax.ppermute(array, axis, [(i, (i + by) % 4) for i in range(4)])


def in_hbm(array):
    return pltpu.with_memory_space_constraint(array, pltpu.HBM)


def swap(array):
    return lax.ppermute(array, "c", [(0, 1), (1, 0)])


def exchange(array):
    return lax.all_to_all(array, ("y", "z"), 0, 0, tiled=True)


def shards(queries, keys, values, fwd_out, out_grad, log_norm, doc_bounds, span_plan, read_lists):
    bf16 = jnp.bfloat16
    f32 = jnp.float32

    kv_out = pl.pallas_call(
        pack_kv_kernel,
        grid=(2,),
        out_shape=jax.ShapeDtypeStruct((4, 4, 2, HALF, HEAD_DIM), bf16),
        in_specs=[pl.BlockSpec((HALF, 4 * HEAD_DIM), lambda y: (0, y))] * 2,
        out_specs=pl.BlockSpec((2, 4, 2, HALF, HEAD_DIM), lambda y: (y, 0, 0, 0, 0)),
        name="pack_kv",
    )(keys, values)
    block = exchange(kv_out.reshape(16, 2, HALF, HEAD_DIM))

    norms = log_norm.reshape(4, HALF, 4, 4).transpose(2, 0, 3, 1).reshape(4, 4, 256)
    wide = pl.BlockSpec((HALF, 16 * HEAD_DIM), lambda y: (0, y))
    q_out = pl.pallas_call(
        pack_q_kernel,
        grid=(4,),
        out_shape=jax.ShapeDtypeStruct((4, 4, PACKED, 256), bf16),
        in_specs=[wide, wide, wide, pl.BlockSpec((4, 4, 256), lambda y: (0, 0, 0))],
        out_specs=pl.BlockSpec((1, 4, PACKED, 256), lambda y: (y, 0, 0, 0)),
        name="pack_q",
    )(queries, out_grad, fwd_out, norms)
    packed = exchange(q_out.reshape(16, PACKED, 256))

    from_next = shift(block, "x", -1)
    from_last = shift(block, "x", 1)
    far_a = shift(from_next[:8], "x", -1)
    far_b = shift(from_last[8:], "x", 1)

    plan, bounds = in_hbm(span_plan), in_hbm(doc_bounds)
    mine = [block, from_next, far_a, far_b, from_last]
    other = [swap(part) for part in mine]
    dq, keep, send = tiles(plan, bounds, packed, mine, other)

    got = swap(send)

    def block_of(slab, half):
        return pl.BlockSpec((1, 4, 2, HEAD_DIM, SPAN), lambda _: (slab, half, 0, 0, 0))

    piece = jax.ShapeDtypeStruct((1, 4, 2, HEAD_DIM, SPAN), bf16)
    via_next, via_last, last_b, next_a = pl.pallas_call(
        functools.partial(add_kernel, 2),
        grid=(1,),
        out_shape=[piece] * 4,
        in_specs=[block_of(*place) for place in ((2, 0), (2, 1), (1, 1), (3, 0)) for _ in range(2)],
        out_specs=[block_of(0, 0)] * 4,
        compiler_params=pltpu.CompilerParams(vmem_limit_bytes=8 * MIB),
        name="first_sums",
    )(*[keep, got] * 4)
    via_next, via_last = shift(via_next, "x", 1), shift(via_last, "x", -1)
    last_b, next_a = shift(last_b, "x", 1), shift(next_a, "x", -1)
    last_a, next_b = pl.pallas_call(
        functools.partial(add_kernel, 3),
        grid=(1,),
        out_shape=[piece] * 2,
        in_specs=[block_of(1, 0)] * 2 + [block_of(0, 0)] + [block_of(3, 1)] * 2 + [block_of(0, 0)],
        out_specs=[block_of(0, 0)] * 2,
        compiler_params=pltpu.CompilerParams(vmem_limit_bytes=6 * MIB),
        name="second_sums",
    )(keep, got, via_next, keep, got, via_last)
    last_a, next_b = shift(last_a, "x", 1), shift(next_b, "x", -1)
    dq_back = exchange(dq).reshape(4, 4, HEAD_DIM, 256)
    slab = pl.BlockSpec((1, 4, 2, HEAD_DIM, SPAN), lambda j: (0, j, 0, 0, 0))
    total = pl.pallas_call(
        final_kernel,
        grid=(2,),
        out_shape=pltpu.HBM((16, 2, HALF, HEAD_DIM), bf16),
        in_specs=[slab] * 2 + [block_of(0, 0)] * 4,
        out_specs=pl.BlockSpec((8, 2, HALF, HEAD_DIM), lambda j: (j, 0, 0, 0)),
        compiler_params=pltpu.CompilerParams(vmem_limit_bytes=8 * MIB),
        name="own_slab",
    )(keep, got, last_a, last_b, next_a, next_b)
    total, dq_back = lax.optimization_barrier((total, dq_back))
    kv_back = exchange(total)
    grad_queries = pl.pallas_call(
        unpack_q_kernel,
        grid=(4,),
        out_shape=jax.ShapeDtypeStruct((HALF, 64 * HEAD_DIM), bf16),
        in_specs=[pl.BlockSpec((1, 4, HEAD_DIM, 256), lambda y: (y, 0, 0, 0))],
        out_specs=wide,
        compiler_params=pltpu.CompilerParams(vmem_limit_bytes=6 * MIB),
        name="unpack_q",
    )(dq_back)
    grad_keys, grad_values = pl.pallas_call(
        unpack_kv_kernel,
        out_shape=[jax.ShapeDtypeStruct((HALF, 8 * HEAD_DIM), bf16)] * 2,
        in_specs=[VMEM],
        out_specs=[VMEM, VMEM],
        compiler_params=pltpu.CompilerParams(vmem_limit_bytes=4 * MIB),
        name="unpack_kv",
    )(kv_back.reshape(4, 4, 2, HALF, HEAD_DIM))
    return (grad_queries, grad_keys, grad_values)


def solution(mesh):
    fine = Mesh(mesh.devices.reshape(4, 4, 2, 4), ROWS)
    rows = P(ROWS, None)
    cp = ("z", "x", "c")
    in_specs = (rows, rows, rows, rows, rows, P(cp, "y"), P(), P(), P(cp, None, None))
    return jax.shard_map(shards, mesh=fine, in_specs=in_specs, out_specs=(rows, rows, rows), check_vma=False)
```
